32 devices in a mesh: dp: 2 (over z_hi), seq: 8 (over y, x, core), head: 2 (over z_lo).
Axes of the slice: x: 2, y: 2, z: 4 (z_hi: 2, z_lo: 2; z = z_hi * 2 + z_lo), core: 2. Of those that a mesh axis runs over, the one named last changes fastest.
Arguments:
- tokens: bfloat16 [6144, 2048], P(('dp', 'seq')), may hold values from -6 to 6
- mix_gain: float32 [2048], replicated, may hold values from 0.1 to 1.9
- w_query: bfloat16 [2048, 1024], P(('dp', 'seq'), 'head'), may hold values from -0.125 to 0.125
- w_key: bfloat16 [2048, 1024], P(('dp', 'seq'), 'head'), may hold values from -0.125 to 0.125
- w_value: bfloat16 [2048, 2048], P(('dp', 'seq'), 'head'), may hold values from -0.125 to 0.125
- w_outgate: bfloat16 [2048, 2048], P(('dp', 'seq'), 'head'), may hold values from -0.125 to 0.125
- w_lowrank: bfloat16 [2048, 16], P(('dp', 'seq')), may hold values from -0.125 to 0.125
- w_rate: bfloat16 [16, 1024], P(None, 'head'), may hold values from -1.5 to 1.5
- rate_bias: float32 [1024], P('head'), may hold values from -1 to 12
- head_gain: float32 [512], replicated, may hold values from 0.1 to 1.9
- w_output: bfloat16 [2048, 2048], P('head', ('dp', 'seq')), may hold values from -0.1875 to 0.1875
- mlp_gain: float32 [2048], replicated, may hold values from 0.1 to 1.9
- w_gate: bfloat16 [2048, 5632], P(('dp', 'seq'), 'head'), may hold values from -0.125 to 0.125
- w_up: bfloat16 [2048, 5632], P(('dp', 'seq'), 'head'), may hold values from -0.125 to 0.125
- w_down: bfloat16 [5632, 2048], P('head', ('dp', 'seq')), may hold values from -0.15625 to 0.15625
- cotangent: bfloat16 [6144, 2048], P(('dp', 'seq')), may hold values from -6 to 6
Outputs:
- result: bfloat16 [6144, 2048], P(('dp', 'seq'))
- grad_tokens: float32 [6144, 2048], P(('dp', 'seq'))
- grad_mix_gain: float32 [2048], replicated
- grad_query: float32 [2048, 1024], P(('dp', 'seq'), 'head')
- grad_key: float32 [2048, 1024], P(('dp', 'seq'), 'head')
- grad_value: float32 [2048, 2048], P(('dp', 'seq'), 'head')
- grad_outgate: float32 [2048, 2048], P(('dp', 'seq'), 'head')
- grad_lowrank: float32 [2048, 16], P(('dp', 'seq'))
- grad_rate: float32 [16, 1024], P(None, 'head')
- grad_rate_bias: float32 [1024], P('head')
- grad_head_gain: float32 [512], replicated
- grad_output: float32 [2048, 2048], P('head', ('dp', 'seq'))
- grad_mlp_gain: float32 [2048], replicated
- grad_gate: float32 [2048, 5632], P(('dp', 'seq'), 'head')
- grad_up: float32 [2048, 5632], P(('dp', 'seq'), 'head')
- grad_down: float32 [5632, 2048], P('head', ('dp', 'seq'))
The draws below stay inside these ranges and needn't reach their ends.
All inputs are finite; a program needn't handle non-finite values.
Results may differ from the reference program's by a relative error of at most 0.015.
The reference program's roundings to bfloat16 on the way count: a program that leaves them out, or rounds other values in their place, can miss the bound.
Values may be sent and summed in bfloat16 or wider, within the bound.
No kernel may reach another device: no remote copies, remote signals or barrier semaphores. Data moves between devices by JAX's collectives and lax.ppermute only.
A program may use at most 168 MiB of HBM per device.

```python
import jax
import jax.numpy as jnp
from jax import lax

D = 2048
NH = 4
KD = 256
VD = 512
FF = 5632
RANK = 16
BLOCK_LEN = 64
KEY = 1024
VAL = 2048
LEN = 3072
TOKENS = 6144
N_DP = 2


def block_scale(own_key, shape, split, smallest, high):
    loudness = 1.0
    for position, shards_of in split:
        draws = jax.random.uniform(jax.random.fold_in(jax.random.fold_in(own_key, 6), position), (shards_of,), jnp.float32, smallest / len(split), high / len(split))
        loudness = loudness * jnp.repeat(jnp.exp(draws), shape[position] // shards_of).reshape((-1,) + (1,) * (len(shape) - 1 - position))
    return loudness


def scatter_about(own_key, extent, width, limit, cuts=(), held_as=jnp.bfloat16):
    loudness = block_scale(own_key, extent, cuts, -0.22, 0.18) if cuts else 1.0
    drawn = jax.random.normal(own_key, extent, jnp.float32) * width * loudness
    return jnp.minimum(jnp.maximum(drawn, -limit), limit).astype(held_as)


def setup_inputs(seed: int = 0) -> dict:
    key_of = jax.random.split(jax.random.key(seed), 17)
    return {
        "tokens": scatter_about(key_of[0], (TOKENS, D), 1.0, 6.0, ((0, 16),)),
        "mix_gain": jnp.clip(1.0 + 0.18 * jax.random.normal(key_of[1], (D,), jnp.float32), 0.1, 1.9),
        "w_query": scatter_about(key_of[2], (D, KEY), D ** -0.5, 0.125, ((0, 16), (1, 2))),
        "w_key": scatter_about(key_of[3], (D, KEY), D ** -0.5, 0.125, ((0, 16), (1, 2))),
        "w_value": scatter_about(key_of[4], (D, VAL), D ** -0.5, 0.125, ((0, 16), (1, 2))),
        "w_outgate": scatter_about(key_of[5], (D, VAL), D ** -0.5, 0.125, ((0, 16), (1, 2))),
        "w_lowrank": scatter_about(key_of[6], (D, RANK), D ** -0.5, 0.125, ((0, 16),)),
        "w_rate": scatter_about(key_of[7], (RANK, KEY), RANK ** -0.5, 1.5, ((1, 2),)),
        "rate_bias": jnp.clip(-1.0 + 13.0 * jax.random.uniform(key_of[8], (KEY,), jnp.float32) ** block_scale(key_of[8], (KEY,), ((0, 2),), -0.2, 0.2), -1.0, 12.0),
        "head_gain": jnp.clip(1.0 + 0.18 * jax.random.normal(key_of[9], (VD,), jnp.float32), 0.1, 1.9),
        "w_output": scatter_about(key_of[10], (VAL, D), (VAL // 2) ** -0.5, 0.1875, ((0, 2), (1, 16))),
        "mlp_gain": jnp.clip(1.0 + 0.18 * jax.random.normal(key_of[11], (D,), jnp.float32), 0.1, 1.9),
        "w_gate": scatter_about(key_of[12], (D, FF), D ** -0.5, 0.125, ((0, 16), (1, 2))),
        "w_up": scatter_about(key_of[13], (D, FF), D ** -0.5, 0.125, ((0, 16), (1, 2))),
        "w_down": scatter_about(key_of[14], (FF, D), (FF // 4) ** -0.5, 0.15625, ((0, 2), (1, 16))),
        "cotangent": scatter_about(key_of[15], (TOKENS, D), 1.0, 6.0, ((0, 16),)),
    }


epsilon = 1e-06
normalizer = 16.0
MATMUL_PRECISION = lax.Precision.HIGHEST

@jax.custom_vjp
def low(v):
    return lax.optimization_barrier(v.astype(jnp.bfloat16)).astype(jnp.float32)

@jax.custom_vjp
def low_back(v):
    return v

def low_keep(v):
    return (low(v), None)

def low_pass(kept, grad):
    return (grad,)

def back_keep(v):
    return (v, None)

def back_low(kept, grad):
    return (low(grad),)
low.defvjp(low_keep, low_pass)
low_back.defvjp(back_keep, back_low)

def matmul(left, right):
    return jnp.dot(left, right, precision=MATMUL_PRECISION)

def rms_norm(x, gain):
    return x * lax.rsqrt(lax.optimization_barrier(jnp.mean(x * x, axis=-1, keepdims=True)) + epsilon) * gain

def head_norm(mixed_output, outgate, gain):
    return rms_norm(mixed_output, gain) * jax.nn.silu(outgate)

def block_step(state_value, pieces):
    query, key, value_rows, decay = pieces
    running = jnp.cumsum(decay, axis=0)
    final_state = running[-1]
    lifted_output = query * jnp.exp(running)
    lowered = key * jnp.exp(-running)
    scores = jnp.einsum('thk,shk->hts', lifted_output, lowered, precision=MATMUL_PRECISION)
    length = decay.shape[0]
    lower = jnp.arange(length)[:, None] >= jnp.arange(length)[None, :]
    scores = jnp.where(lower[None], scores, 0.0)
    mixed_output = jnp.einsum('wlc,lcg->wlg', lifted_output, state_value, precision=MATMUL_PRECISION)
    mixed_output = mixed_output + jnp.einsum('hts,shv->thv', scores, value_rows, precision=MATMUL_PRECISION)
    carried_state = key * jnp.exp(final_state[None] - running)
    state_value = jnp.exp(final_state)[:, :, None] * state_value + jnp.einsum('nps,npx->psx', carried_state, value_rows, precision=MATMUL_PRECISION)
    return (state_value, mixed_output)

def block_scan(query, key, value_rows, decay, state_value):
    length, heads, kdim = query.shape
    vdim = value_rows.shape[2]
    count = length // BLOCK_LEN
    pieces = (query.reshape(count, BLOCK_LEN, heads, kdim), key.reshape(count, BLOCK_LEN, heads, kdim), value_rows.reshape(count, BLOCK_LEN, heads, vdim), decay.reshape(count, BLOCK_LEN, heads, kdim))
    state_value, mixed_output = lax.scan(jax.checkpoint(block_step), state_value, pieces)
    return (state_value, mixed_output.reshape(length, heads, vdim))

def layer(inputs, mix_gain, w_query, w_key, w_value, w_outgate, w_lowrank, w_rate, rate_bias, head_gain, w_output, mlp_gain, w_gate, w_up, w_down):
    length = inputs.shape[0]
    normed = low(rms_norm(inputs, mix_gain))
    query = low_back(matmul(normed, w_query)).reshape(length, NH, KD) * KD ** (-0.5)
    key = low_back(matmul(normed, w_key)).reshape(length, NH, KD)
    value_rows = low_back(matmul(normed, w_value)).reshape(length, NH, VD)
    outgate = low_back(matmul(normed, w_outgate)).reshape(length, NH, VD)
    rank_part = low(low_back(matmul(normed, w_lowrank)))
    logit = low_back(matmul(rank_part, w_rate) + rate_bias)
    decay = (jax.nn.log_sigmoid(logit) / normalizer).reshape(length, NH, KD)
    zeros = jnp.zeros((NH, KD, VD), jnp.float32)
    _, mixed_output = block_scan(query, key, value_rows, decay, zeros)
    gated = low(head_norm(mixed_output, outgate, head_gain).reshape(length, VAL))
    middle = inputs + low_back(matmul(gated, w_output))
    normed2 = low(rms_norm(middle, mlp_gain))
    gate = low_back(matmul(normed2, w_gate))
    upward = low_back(matmul(normed2, w_up))
    hidden = low(jax.nn.silu(gate) * upward)
    return middle + low_back(matmul(hidden, w_down))

def reference(tokens, mix_gain, w_query, w_key, w_value, w_outgate, w_lowrank, w_rate, rate_bias, head_gain, w_output, mlp_gain, w_gate, w_up, w_down, cotangent):
    weights = tuple((weight.astype(jnp.float32) for weight in (mix_gain, w_query, w_key, w_value, w_outgate, w_lowrank, w_rate, rate_bias, head_gain, w_output, mlp_gain, w_gate, w_up, w_down)))
    inputs = tokens.astype(jnp.float32).reshape(N_DP, LEN, D)

    def whole(inputs, *weights):
        return lax.map(lambda sequence: layer(sequence, *weights), inputs)
    outcome, pullback = jax.vjp(whole, inputs, *weights)
    grads = pullback(cotangent.astype(jnp.float32).reshape(N_DP, LEN, D))
    return (outcome.reshape(TOKENS, D).astype(jnp.bfloat16), grads[0].reshape(TOKENS, D), grads[1], grads[2], grads[3], grads[4], grads[5], grads[6], grads[7], grads[8], grads[9], grads[10], grads[11], grads[12], grads[13], grads[14])
```

```python
import jax
import jax.numpy as jnp
from jax import lax
from jax.sharding import PartitionSpec as P

KD = 256
VD = 512
BLOCK_LEN = 64

epsilon = 1e-06
normalizer = 16.0
MATMUL_PRECISION = lax.Precision.HIGHEST
BF16 = jnp.bfloat16
F32 = jnp.float32
CORE = 1


def swap(x, axis, bit=1):
    count = lax.axis_size(axis)
    return lax.ppermute(x, axis, [(i, i ^ bit) for i in range(count)])


def matmul(left, right):
    return jnp.dot(left, right, preferred_element_type=F32)


def inner(left, right):
    return lax.dot_general(left, right, (((0,), (0,)), ((), ())), preferred_element_type=F32)


def times_back(grad, weight):
    return lax.dot_general(grad, weight, (((1,), (1,)), ((), ())), preferred_element_type=F32)


def rms_norm(x, gain):
    return x * lax.rsqrt(jnp.mean(x * x, axis=-1, keepdims=True) + epsilon) * gain


def head_norm(mixed_output, outgate, gain):
    return rms_norm(mixed_output, gain) * jax.nn.silu(outgate)


def swiglu(gate, upward):
    return jax.nn.silu(gate) * upward


def block_step(state_value, pieces):
    query, key, value_rows, decay = pieces
    running = jnp.cumsum(decay, axis=0)
    final_state = running[-1]
    lifted_output = query * jnp.exp(running)
    lowered = key * jnp.exp(-running)
    scores = jnp.einsum("thk,shk->hts", lifted_output, lowered, precision=MATMUL_PRECISION)
    length = decay.shape[0]
    lower = jnp.arange(length)[:, None] >= jnp.arange(length)[None, :]
    scores = jnp.where(lower[None], scores, 0.0)
    mixed_output = jnp.einsum(
        "wlc,lcg->wlg", lifted_output, state_value, precision=MATMUL_PRECISION
    )
    mixed_output = mixed_output + jnp.einsum(
        "hts,shv->thv", scores, value_rows, precision=MATMUL_PRECISION
    )
    carried_state = key * jnp.exp(final_state[None] - running)
    state_value = jnp.exp(final_state)[:, :, None] * state_value + jnp.einsum(
        "nps,npx->psx", carried_state, value_rows, precision=MATMUL_PRECISION
    )
    return (state_value, mixed_output)


def block_scan(query, key, value_rows, decay, state_value):
    length, heads, kdim = query.shape
    vdim = value_rows.shape[2]
    count = length // BLOCK_LEN
    pieces = (
        query.reshape(count, BLOCK_LEN, heads, kdim),
        key.reshape(count, BLOCK_LEN, heads, kdim),
        value_rows.reshape(count, BLOCK_LEN, heads, vdim),
        decay.reshape(count, BLOCK_LEN, heads, kdim),
    )
    state_value, mixed_output = lax.scan(jax.checkpoint(block_step), state_value, pieces)
    return (state_value, mixed_output.reshape(length, heads, vdim))


def local_mixer(query, key, value_rows, decay):
    scaled = query * KD ** (-0.5)
    zeros = jnp.zeros((query.shape[1], KD, value_rows.shape[2]), F32)
    state_end, mixed_output = block_scan(scaled, key, value_rows, decay, zeros)
    running = jnp.cumsum(decay, axis=0)
    return (state_end, mixed_output, scaled * jnp.exp(running), jnp.exp(running[-1]))


def chip_bits():
    bits, bit = [], 2
    while bit < lax.axis_size("seq"):
        bits.append(bit)
        bit *= 2
    return bits


def paths():
    bits = chip_bits()
    return bits, bits[::-1]


def spread(half, path):
    for bit in path:
        half = jnp.concatenate([half, swap(half, "seq", bit)], 0)
    return half


def order():
    blocks = []
    chip = lax.axis_index("seq") // 2
    dp = lax.axis_index("dp")
    chips = lax.axis_size("seq") // 2
    for away in range(2):
        for half, path in enumerate(paths()):
            near = [0]
            for bit in path:
                near = near + [place ^ (bit // 2) for place in near]
            blocks += [(((dp ^ away) * chips + (chip ^ place)) * 2 + half) for place in near]
    return blocks


def gather(first, second):
    far_first, far_second = swap(first, "dp"), swap(second, "dp")
    one, two = paths()
    return jnp.concatenate(
        [spread(first, one), spread(second, two), spread(far_first, one), spread(far_second, two)],
        0,
    )


def collect(part, path):
    for bit in path[::-1]:
        length = part.shape[0] // 2
        sent = swap(part[length:].astype(BF16), "seq", bit)
        part = part[:length].astype(F32) + sent.astype(F32)
    return part


def scatter(left, right):
    quarter = left.shape[1] // 4
    one, two = paths()
    sums = []
    for i, path in ((2, one), (3, two), (0, one), (1, two)):
        grad = inner(left[:, i * quarter : (i + 1) * quarter], right).astype(BF16)
        sums.append(collect(grad, path))
    far = [swap(part.astype(BF16), "dp") for part in sums[:2]]
    return [near + part.astype(F32) for near, part in zip(sums[2:], far)]


def both(x, core):
    other = swap(x, "seq", CORE)
    return jnp.concatenate([jnp.where(core == 0, x, other), jnp.where(core == 0, other, x)], 0)


def add_up(part, core):
    rows = part.shape[0] // 2
    mine = jnp.where(core == 0, part[:rows], part[rows:])
    theirs = jnp.where(core == 0, part[rows:], part[:rows])
    mine = mine + swap(theirs.astype(BF16), "seq", CORE).astype(F32)
    mine = mine.astype(BF16)
    return mine.astype(F32) + swap(mine, "head").astype(F32)


def incoming(edge, state, reverse=False):
    chips = lax.axis_size("seq") // 2
    chip = lax.axis_index("seq") // 2
    low = state.astype(BF16)

    def move(x, by):
        if reverse:
            by = -by
        pairs = []
        for i in range(chips):
            if 0 <= i + by < chips:
                for c in range(2):
                    pairs.append((2 * i + c, 2 * (i + by) + c))
        return lax.ppermute(x, "seq", pairs)

    total = jnp.zeros_like(state)
    faded = None
    edges = edge
    for by in range(1, chips):
        there = move(low, by).astype(F32)
        if by == 1:
            total = there
        else:
            total = total + faded[:, None] * there
        if by < chips - 1:
            gone = move(edge, by)
            faded = gone if faded is None else faded * gone
    return total


def body(
    tokens,
    mix_gain,
    w_query,
    w_key,
    w_value,
    w_outgate,
    w_lowrank,
    w_rate,
    rate_bias,
    head_gain,
    w_output,
    mlp_gain,
    w_gate,
    w_up,
    w_down,
    cotangent,
):
    core = lax.axis_index("seq") % 2
    blocks = order()
    place_of = jnp.stack(blocks)
    back_place = jnp.argsort(place_of)

    wide = tokens.shape[1] // len(blocks)

    def local(x):
        return jnp.concatenate(
            [lax.dynamic_slice_in_dim(x, b * wide, wide, x.ndim - 1) for b in blocks], x.ndim - 1
        )

    def whole(x):
        return jnp.concatenate(
            [
                lax.dynamic_slice_in_dim(x, back_place[i] * wide, wide, x.ndim - 1)
                for i in range(len(blocks))
            ],
            x.ndim - 1,
        )

    def split(w):
        half = w.shape[1] // 2
        mine = jnp.where(core == 0, w[:, :half], w[:, half:])
        theirs = jnp.where(core == 0, w[:, half:], w[:, :half])
        return mine, theirs

    def own_columns(weights):
        pairs = [split(w) for w in weights]
        mine = jnp.concatenate([p[0] for p in pairs], 1)
        got = swap(jnp.concatenate([p[1] for p in pairs], 1), "seq", CORE)
        return jnp.where(core == 0, mine, got), jnp.where(core == 0, got, mine)

    mixer_halves = own_columns([w_query, w_key, w_value, w_outgate])
    output_halves = own_columns([w_output.T])
    up_halves = own_columns([w_gate, w_up])
    down_halves = own_columns([w_down.T])
    low_full = lax.all_gather(w_lowrank.T, ("dp", "seq"), axis=1, tiled=True)
    w_mixer = gather(*mixer_halves)
    w_out = gather(*output_halves)
    w_gateup = gather(*up_halves)
    w_dn = gather(*down_halves)

    low_local = local(low_full)
    gain1, gain2 = local(mix_gain[None])[0], local(mlp_gain[None])[0]
    cot = local(cotangent)
    cot_both = both(cot, core)
    inputs = local(tokens).astype(F32)
    length = 2 * tokens.shape[0]

    normed, norm_back = jax.vjp(rms_norm, inputs, gain1)
    normed_own = normed.astype(BF16)
    normed_low = both(normed_own, core)
    projected = matmul(normed_low, w_mixer)
    query = projected[:, :KD].reshape(length, 1, KD)
    key = projected[:, KD : 2 * KD].reshape(length, 1, KD)
    value_rows = projected[:, 2 * KD : 2 * KD + VD].reshape(length, 1, VD)
    outgate = projected[:, 2 * KD + VD :]
    rank_part = times_back(normed_low, low_local).astype(BF16)
    rate = jnp.where(core == 0, w_rate[:, :KD], w_rate[:, KD:])
    bias = jnp.where(core == 0, rate_bias[:KD], rate_bias[KD:])
    logit = matmul(rank_part, rate) + bias
    decay = (jax.nn.log_sigmoid(logit) / normalizer).reshape(length, 1, KD)
    (state_end, local_output, lifted_output, edge), mixer_back = jax.vjp(
        local_mixer, query, key, value_rows, decay
    )
    incoming_state = incoming(edge[0], state_end[0])
    lifted = lifted_output[:, 0]
    mixed_output = local_output[:, 0] + jnp.dot(
        lifted, incoming_state, precision=MATMUL_PRECISION
    )
    gated, gated_back = jax.vjp(head_norm, mixed_output, outgate, head_gain)
    gated_low = gated.astype(BF16)
    middle = inputs + add_up(times_back(gated_low, w_out), core)
    normed2, norm2_back = jax.vjp(rms_norm, middle, gain2)
    normed2_low = both(normed2.astype(BF16), core)
    gateup = matmul(normed2_low, w_gateup)
    half = gateup.shape[1] // 2
    hidden, swiglu_back = jax.vjp(swiglu, gateup[:, :half], gateup[:, half:])
    hidden_low = hidden.astype(BF16)
    feed = add_up(times_back(hidden_low, w_dn), core)
    result = whole((middle + feed).astype(BF16))

    grad_down = scatter(cot_both, hidden_low)
    grad_hidden = matmul(cot_both, w_dn)
    gate_grad, upward_grad = swiglu_back(grad_hidden)
    gateup_low = jnp.concatenate([gate_grad.astype(BF16), upward_grad.astype(BF16)], 1)
    grad_normed2 = add_up(times_back(gateup_low, w_gateup), core)
    grad_gateup = scatter(normed2_low, gateup_low)
    middle_grad, grad_mlp_gain = norm2_back(grad_normed2)
    grad_middle = cot.astype(F32) + middle_grad
    middle_low = both(grad_middle.astype(BF16), core)
    grad_gated = matmul(middle_low, w_out)
    grad_output = scatter(middle_low, gated_low)
    mixed_gradient, outgate_grad, head_gain_part = gated_back(grad_gated)
    lifted_gradient = lax.dot_general(
        mixed_gradient, incoming_state, (((1,), (1,)), ((), ())), precision=MATMUL_PRECISION
    )
    own_contribution = lax.dot_general(
        lifted, mixed_gradient, (((0,), (0,)), ((), ())), precision=MATMUL_PRECISION
    )
    outgoing = incoming(edge[0], own_contribution, reverse=True)
    grad_edge = jnp.sum(incoming_state * outgoing, axis=1)
    query_grad, key_grad, value_grad, decay_grad = mixer_back(
        (outgoing[None], mixed_gradient[:, None], lifted_gradient[:, None], grad_edge[None])
    )
    mixer_low = jnp.concatenate(
        [
            query_grad.reshape(length, -1).astype(BF16),
            key_grad.reshape(length, -1).astype(BF16),
            value_grad.reshape(length, -1).astype(BF16),
            outgate_grad.astype(BF16),
        ],
        1,
    )
    logit_low = (decay_grad.reshape(length, -1) * jax.nn.sigmoid(-logit) / normalizer).astype(BF16)
    grad_rate = inner(rank_part, logit_low)
    grad_rate_bias = jnp.sum(logit_low.astype(F32), axis=0)
    rank_part_grad = times_back(logit_low, rate)
    rank_own = add_up(rank_part_grad, core).astype(BF16)
    normed_sum = add_up(times_back(mixer_low, w_mixer), core)
    grad_mixer = scatter(normed_low, mixer_low)
    grad_lowrank = whole(inner(rank_own, normed_own))
    grad_normed = normed_sum + matmul(rank_own, low_local)
    inputs_grad, grad_mix_gain = norm_back(grad_normed)
    grad_tokens = whole(grad_middle + inputs_grad)

    def own_rows(halves):
        mine = jnp.where(core == 0, halves[0], halves[1])
        theirs = jnp.where(core == 0, halves[1], halves[0])
        got = swap(theirs.astype(BF16), "seq", CORE).astype(F32)
        return jnp.where(core == 0, mine, got), jnp.where(core == 0, got, mine)

    def columns(pair, start, width):
        return jnp.concatenate([part[:, start : start + width] for part in pair], 1)

    mixer_pair = own_rows(grad_mixer)
    sum_query = columns(mixer_pair, 0, KD)
    sum_key = columns(mixer_pair, KD, KD)
    sum_value = columns(mixer_pair, 2 * KD, VD)
    sum_outgate = columns(mixer_pair, 2 * KD + VD, VD)
    output_pair = own_rows(grad_output)
    sum_output = columns(output_pair, 0, VD).T
    gateup_pair = own_rows(grad_gateup)
    sum_gate = columns(gateup_pair, 0, half)
    sum_up = columns(gateup_pair, half, half)
    down_pair = own_rows(grad_down)
    sum_down = columns(down_pair, 0, half).T

    zero = jnp.zeros_like(grad_rate)
    wide_rate = jnp.where(
        core == 0,
        jnp.concatenate([grad_rate, zero], 1),
        jnp.concatenate([zero, grad_rate], 1),
    )
    wide_bias = jnp.where(
        core == 0,
        jnp.concatenate([grad_rate_bias, zero[0]]),
        jnp.concatenate([zero[0], grad_rate_bias]),
    )
    sum_mix_gain, sum_mlp_gain, sum_rate, sum_rate_bias, sum_low = lax.psum(
        (
            whole(grad_mix_gain[None])[0],
            whole(grad_mlp_gain[None])[0],
            wide_rate,
            wide_bias,
            grad_lowrank,
        ),
        ("dp", "seq"),
    )
    sum_head_gain = lax.psum(head_gain_part, ("dp", "seq", "head"))
    spot = lax.axis_index("dp") * lax.axis_size("seq") + lax.axis_index("seq")
    sum_lowrank = lax.dynamic_slice_in_dim(sum_low, spot * wide, wide, 1).T
    return (
        result,
        grad_tokens,
        sum_mix_gain,
        sum_query,
        sum_key,
        sum_value,
        sum_outgate,
        sum_lowrank,
        sum_rate,
        sum_rate_bias,
        sum_head_gain,
        sum_output,
        sum_mlp_gain,
        sum_gate,
        sum_up,
        sum_down,
    )


def solution(mesh):
    rows = P(("dp", "seq"), None)
    in_columns = P(("dp", "seq"), "head")
    in_rows = P("head", ("dp", "seq"))
    in_specs = (
        rows,
        P(),
        in_columns,
        in_columns,
        in_columns,
        in_columns,
        rows,
        P(None, "head"),
        P("head"),
        P(),
        in_rows,
        P(),
        in_columns,
        in_columns,
        in_rows,
        rows,
    )
    out_specs = (
        rows,
        rows,
        P(),
        in_columns,
        in_columns,
        in_columns,
        in_columns,
        rows,
        P(None, "head"),
        P("head"),
        P(),
        in_rows,
        P(),
        in_columns,
        in_columns,
        in_rows,
    )
    return jax.shard_map(body, mesh=mesh, in_specs=in_specs, out_specs=out_specs, check_vma=False)
```

```python
import functools

import jax
import jax.numpy as jnp
from jax import lax
from jax.experimental import pallas as pl
from jax.experimental.pallas import tpu as pltpu
from jax.sharding import PartitionSpec as P

KD = 256
VD = 512
BLOCK_LEN = 64

epsilon = 1e-06
normalizer = 16.0
MATMUL_PRECISION = lax.Precision.HIGHEST
BF16 = jnp.bfloat16
F32 = jnp.float32
CORE = 1


def swap(x, axis, bit=1):
    count = lax.axis_size(axis)
    return lax.ppermute(x, axis, [(i, i ^ bit) for i in range(count)])


def matmul(left, right):
    return jnp.dot(left, right, preferred_element_type=F32)


def inner(left, right):
    return lax.dot_general(left, right, (((0,), (0,)), ((), ())), preferred_element_type=F32)


def times_back(grad, weight):
    return lax.dot_general(grad, weight, (((1,), (1,)), ((), ())), preferred_element_type=F32)


def rms_norm(x, gain):
    return x * lax.rsqrt(jnp.mean(x * x, axis=-1, keepdims=True) + epsilon) * gain


def head_norm(mixed_output, outgate, gain):
    return rms_norm(mixed_output, gain) * jax.nn.silu(outgate)


def swiglu(gate, upward):
    return jax.nn.silu(gate) * upward


def dot(a, b, contract, passes=1):
    dims = ((contract[0],), (contract[1],)), ((), ())

    def once(x, y):
        return lax.dot_general(x, y, dims, preferred_element_type=F32)

    high_a, high_b = a.astype(BF16), b.astype(BF16)
    total = once(high_a, high_b)
    if passes > 1:
        low_a = (a - high_a.astype(F32)).astype(BF16)
        low_b = (b - high_b.astype(F32)).astype(BF16)
        total = total + (once(high_a, low_b) + once(low_a, high_b))
    return total


def triangle(size):
    rows = lax.broadcasted_iota(jnp.int32, (size, size), 0)
    columns = lax.broadcasted_iota(jnp.int32, (size, size), 1)
    return rows >= columns


def block_terms(query, key, decay):
    size = decay.shape[0]
    ones = jnp.where(triangle(size), 1.0, 0.0)
    running = lax.dot_general(
        ones, decay, (((1,), (0,)), ((), ())), precision=MATMUL_PRECISION, preferred_element_type=F32
    )
    final = running[size - 1 : size]
    rise, fall, rest = jnp.exp(running), jnp.exp(-running), jnp.exp(final - running)
    return query * (KD**-0.5) * rise, key * fall, key * rest, rise, fall, rest, final


PASSES = 1


def forward_kernel(q_ref, k_ref, v_ref, d_ref, out_ref, lifted_ref, states_ref, end_ref, edge_ref, prefix_ref, state, before):
    @pl.when(pl.program_id(0) == 0)
    def _():
        state[...] = jnp.zeros_like(state)
        before[...] = jnp.zeros_like(before)

    lifted, lowered, carried, _, _, _, final = block_terms(q_ref[...], k_ref[...], d_ref[...])
    value = v_ref[...]
    scores = dot(lifted, lowered, (1, 1), PASSES)
    scores = jnp.where(triangle(scores.shape[0]), scores, 0.0)
    held = state[...]
    out_ref[...] = dot(scores, value, (1, 0), PASSES) + dot(lifted, held, (1, 1), PASSES)
    reach = jnp.exp(before[0:1])
    lifted_ref[...] = lifted * reach
    prefix_ref[...] = reach[None]
    states_ref[...] = held[None]
    new = held * jnp.exp(final) + dot(value, carried, (0, 0), PASSES)
    state[...] = new
    before[0:1] = before[0:1] + final
    end_ref[...] = new
    edge_ref[...] = jnp.exp(before[0:1])


def backward_kernel(q_ref, k_ref, v_ref, d_ref, grad_ref, states_ref, prefix_ref, in_ref, out_ref, mixer_ref, decay_ref, state):
    @pl.when(pl.program_id(0) == 0)
    def _():
        state[...] = out_ref[...]

    lifted, lowered, carried, rise, fall, rest, final = block_terms(q_ref[...], k_ref[...], d_ref[...])
    value, grad = v_ref[...], grad_ref[...]
    later = state[...]
    held = states_ref[0] + in_ref[...] * prefix_ref[0]
    lower = triangle(value.shape[0])
    scores = jnp.where(lower, dot(lifted, lowered, (1, 1), PASSES), 0.0)
    grad_scores = jnp.where(lower, dot(grad, value, (1, 1), PASSES), 0.0)
    grad_value = dot(scores, grad, (0, 0), PASSES) + dot(carried, later, (1, 1), PASSES)
    grad_lifted = dot(grad, held, (1, 0), PASSES) + dot(grad_scores, lowered, (1, 0), PASSES)
    grad_lowered = dot(grad_scores, lifted, (0, 0), PASSES)
    grad_carried = dot(value, later, (1, 0), PASSES)
    mixer_ref[:, :KD] = (grad_lifted * rise * (KD**-0.5)).astype(BF16)
    mixer_ref[:, KD : 2 * KD] = (grad_lowered * fall + grad_carried * rest).astype(BF16)
    mixer_ref[:, 2 * KD :] = grad_value.astype(BF16)
    through = carried * grad_carried
    change = lifted * grad_lifted - lowered * grad_lowered - through
    fade = jnp.exp(final)
    last = jnp.sum(through, axis=0, keepdims=True) + fade * jnp.sum(held * later, axis=0, keepdims=True)
    ones = jnp.where(lower, 1.0, 0.0)
    decay_ref[...] = last + lax.dot_general(
        ones, change, (((0,), (0,)), ((), ())), precision=MATMUL_PRECISION, preferred_element_type=F32
    )
    state[...] = later * fade + dot(grad, lifted, (0, 0), PASSES)


def mixer_forward(projected, decay):
    length = decay.shape[0]
    count = length // BLOCK_LEN
    row = lambda i: (i, 0)
    fixed = lambda i: (0, 0)
    return pl.pallas_call(
        forward_kernel,
        grid=(count,),
        in_specs=[
            pl.BlockSpec((BLOCK_LEN, KD), lambda i: (i, 0)),
            pl.BlockSpec((BLOCK_LEN, KD), lambda i: (i, 1)),
            pl.BlockSpec((BLOCK_LEN, VD), lambda i: (i, 1)),
            pl.BlockSpec((BLOCK_LEN, KD), row),
        ],
        out_specs=[
            pl.BlockSpec((BLOCK_LEN, VD), row),
            pl.BlockSpec((BLOCK_LEN, KD), row),
            pl.BlockSpec((1, VD, KD), lambda i: (i, 0, 0)),
            pl.BlockSpec((VD, KD), fixed),
            pl.BlockSpec((1, KD), fixed),
            pl.BlockSpec((1, 1, KD), lambda i: (i, 0, 0)),
        ],
        out_shape=[
            jax.ShapeDtypeStruct((length, VD), F32),
            jax.ShapeDtypeStruct((length, KD), F32),
            jax.ShapeDtypeStruct((count, VD, KD), F32),
            jax.ShapeDtypeStruct((VD, KD), F32),
            jax.ShapeDtypeStruct((1, KD), F32),
            jax.ShapeDtypeStruct((count, 1, KD), F32),
        ],
        scratch_shapes=[pltpu.VMEM((VD, KD), F32), pltpu.VMEM((8, KD), F32)],
        compiler_params=pltpu.CompilerParams(
            dimension_semantics=("arbitrary",), vmem_limit_bytes=32 * 2**20
        ),
        name="mixer_forward",
    )(projected, projected, projected, decay)


def mixer_backward(projected, decay, grad, states, prefix, earlier, later):
    length = decay.shape[0]
    count = length // BLOCK_LEN
    row = lambda i: (count - 1 - i, 0)
    fixed = lambda i: (0, 0)
    return pl.pallas_call(
        backward_kernel,
        grid=(count,),
        in_specs=[
            pl.BlockSpec((BLOCK_LEN, KD), lambda i: (count - 1 - i, 0)),
            pl.BlockSpec((BLOCK_LEN, KD), lambda i: (count - 1 - i, 1)),
            pl.BlockSpec((BLOCK_LEN, VD), lambda i: (count - 1 - i, 1)),
            pl.BlockSpec((BLOCK_LEN, KD), row),
            pl.BlockSpec((BLOCK_LEN, VD), row),
            pl.BlockSpec((1, VD, KD), lambda i: (count - 1 - i, 0, 0)),
            pl.BlockSpec((1, 1, KD), lambda i: (count - 1 - i, 0, 0)),
            pl.BlockSpec((VD, KD), fixed),
            pl.BlockSpec((VD, KD), fixed),
        ],
        out_specs=[
            pl.BlockSpec((BLOCK_LEN, 2 * KD + VD), row),
            pl.BlockSpec((BLOCK_LEN, KD), row),
        ],
        out_shape=[
            jax.ShapeDtypeStruct((length, 2 * KD + VD), BF16),
            jax.ShapeDtypeStruct((length, KD), F32),
        ],
        scratch_shapes=[pltpu.VMEM((VD, KD), F32)],
        compiler_params=pltpu.CompilerParams(
            dimension_semantics=("arbitrary",), vmem_limit_bytes=32 * 2**20
        ),
        name="mixer_backward",
    )(projected, projected, projected, decay, grad, states, prefix, earlier, later)


def chip_bits():
    bits, bit = [], 2
    while bit < lax.axis_size("seq"):
        bits.append(bit)
        bit *= 2
    return bits


def tie(arrays, *first):
    return lax.optimization_barrier((arrays, first))[0]


def hop(x, step):
    bits = chip_bits()
    there = (bits[step], bits[-1 - step])
    count = lax.axis_size("seq")
    return lax.ppermute(x, "seq", [(i, i ^ there[i % 2]) for i in range(count)])


def place_in(core_order):
    count = len(chip_bits())
    return sum(((core_order >> k) & 1) << (count - 1 - k) for k in range(count))


def same_order(parts, core):
    return [
        x if place_in(i) == i else jnp.where(core == 0, x, parts[place_in(i)])
        for i, x in enumerate(parts)
    ]


class Spread:
    def __init__(self, rows):
        self.parts = [rows]
        self.steps = 0

    def load(self):
        return self.parts[0] if len(self.parts) == 1 else jnp.concatenate(self.parts, 0)

    def take(self, got):
        rows = self.parts[0].shape[0]
        count = len(self.parts)
        self.parts = self.parts + [got[i * rows : (i + 1) * rows] for i in range(count)]
        self.steps += 1


class Collect:
    def __init__(self, rows):
        self.rows = rows
        self.steps = 0

    def load(self):
        return self.rows[self.rows.shape[0] // 2 :].astype(BF16)

    def take(self, got):
        self.rows = self.rows[: self.rows.shape[0] // 2].astype(F32) + got.astype(F32)
        self.steps += 1


class Plane:
    def __init__(self, plan, reverse=False):
        names = sorted({name for slot in plan for name, _ in slot}, key=str(plan).index)
        steps = len(chip_bits())
        self.plan = plan if steps == 2 else [[(n, i)] for n in names for i in range(steps)]
        self.phases = {}
        self.reverse = reverse
        self.done = []

    def slot(self, *first):
        now = self.plan[len(self.done)]
        loads = [self.phases[name].load() for name, _ in now]
        if len(self.done) >= 2:
            first = first + (self.done[-2],)
        if first:
            loads = tie(loads, *first)
        landed = []
        for (name, i), x in zip(now, loads):
            got = hop(x, len(chip_bits()) - 1 - i if self.reverse else i)
            self.phases[name].take(got)
            landed.append(got)
        self.done.append(landed)

    def until(self, *names):
        while any(self.phases[name].steps < len(chip_bits()) for name in names):
            self.slot()


def order():
    chip, dp = lax.axis_index("seq") // 2, lax.axis_index("dp")
    near = [0]
    for bit in chip_bits():
        near = near + [place ^ (bit // 2) for place in near]
    chips = len(near)
    return [(dp ^ away) * chips + (chip ^ place) for away in range(2) for place in near]


def reorder_kernel(count, index_ref, *refs):
    half = len(refs) // 2
    for source, target in zip(refs[:half], refs[half:]):
        width = source.shape[1] // count
        for i in range(count):
            start = pl.multiple_of(index_ref[i] * width, width)
            target[:, i * width : (i + 1) * width] = source[:, pl.ds(start, width)]


def reorder(index, *arrays):
    count = index.shape[0]
    rows, columns = arrays[0].shape
    if (columns // count) % 128:
        moved = [
            jnp.take(x.reshape(rows, count, -1), index, axis=1).reshape(rows, columns)
            for x in arrays
        ]
        return moved
    step = rows // 3 if rows % 48 == 0 else rows
    spec = pl.BlockSpec((step, columns), lambda i, _: (i, 0))
    return pl.pallas_call(
        functools.partial(reorder_kernel, count),
        grid_spec=pltpu.PrefetchScalarGridSpec(
            num_scalar_prefetch=1,
            grid=(rows // step,),
            in_specs=[spec] * len(arrays),
            out_specs=[spec] * len(arrays),
        ),
        out_shape=[jax.ShapeDtypeStruct(x.shape, x.dtype) for x in arrays],
        compiler_params=pltpu.CompilerParams(
            dimension_semantics=("arbitrary",), vmem_limit_bytes=32 * 2**20
        ),
        name="reorder",
    )(index, *arrays)


def core_order(x, core):
    count = 2 * 2 ** len(chip_bits())
    parts = jnp.split(x, count, 1)
    half = count // 2
    return jnp.concatenate(same_order(parts[:half], core) + same_order(parts[half:], core), 1)


def halves(pairs):
    half = pairs[0][0].shape[1] // 2

    def part(i):
        grads = [inner(left[:, i * half : (i + 1) * half], right) for left, right in pairs]
        return jnp.concatenate([grad.astype(BF16) for grad in grads], 1)

    return Collect(part(1)), Collect(part(0))


def both(x, core):
    other = swap(x, "seq", CORE)
    return jnp.concatenate([jnp.where(core == 0, x, other), jnp.where(core == 0, other, x)], 0)


def core_sum(part, core):
    rows = part.shape[0] // 2
    mine = jnp.where(core == 0, part[:rows], part[rows:])
    theirs = jnp.where(core == 0, part[rows:], part[:rows])
    mine = mine + swap(theirs.astype(BF16), "seq", CORE).astype(F32)
    return mine.astype(BF16)


def add_up(part, core):
    mine = core_sum(part, core)
    return mine.astype(F32) + swap(mine, "head").astype(F32)


def incoming(edge, state, reverse=False):
    chips = lax.axis_size("seq") // 2
    rows = state.shape[0]
    high = edge.astype(BF16)
    low = (edge - high.astype(F32)).astype(BF16)
    edges = jnp.pad(jnp.concatenate([high, low], 0), ((0, 14), (0, 0)))
    packed = jnp.concatenate([state.astype(BF16), edges], 0)

    def move(by):
        by = -by if reverse else by
        pairs = []
        for i in range(chips):
            if 0 <= i + by < chips:
                for c in range(2):
                    pairs.append((2 * i + c, 2 * (i + by) + c))
        return lax.ppermute(packed, "seq", pairs).astype(F32)

    total, faded = jnp.zeros_like(state), None
    for by in range(1, chips):
        there = move(by)
        gone = there[rows : rows + 1] + there[rows + 1 : rows + 2]
        if by == 1:
            total, faded = there[:rows], gone
        else:
            total, faded = total + faded * there[:rows], faded * gone
    return total


def body(
    tokens,
    mix_gain,
    w_query,
    w_key,
    w_value,
    w_outgate,
    w_lowrank,
    w_rate,
    rate_bias,
    head_gain,
    w_output,
    mlp_gain,
    w_gate,
    w_up,
    w_down,
    cotangent,
):
    core = lax.axis_index("seq") % 2
    blocks = order()
    wide = tokens.shape[1] // (2 * len(blocks))
    place_of = jnp.stack(blocks).astype(jnp.int32)
    places = jnp.arange(len(blocks), dtype=jnp.int32)
    back_place = jnp.sum(
        jnp.where(place_of[None] == places[:, None], places[None], 0), axis=1, dtype=jnp.int32
    )

    def split(w):
        half = w.shape[1] // 2
        mine = jnp.where(core == 0, w[:, :half], w[:, half:])
        theirs = jnp.where(core == 0, w[:, half:], w[:, :half])
        return mine, theirs

    def own_columns(weights, shared=()):
        pairs = [split(w) for w in weights] + [(w, w) for w in shared]
        mine = jnp.concatenate([p[0] for p in pairs], 1)
        got = swap(jnp.concatenate([p[1] for p in pairs], 1), "seq", CORE)
        return jnp.concatenate(
            [jnp.where(core == 0, mine, got), jnp.where(core == 0, got, mine)], 0
        )

    plane = Plane(
        [
            [("mixer", 0)],
            [("two", 0)],
            [("mixer", 1)],
            [("two", 1)],
            [("far mixer", 0)],
            [("three", 0)],
            [("far mixer", 1)],
            [("three", 1), ("far two", 0)],
            [("down", 0)],
            [("far two", 1), ("far three", 0)],
            [("down", 1), ("far down", 0)],
            [("far three", 1)],
            [("far down", 1)],
        ]
    )
    phases = plane.phases

    def gathered(name, start, width):
        near = same_order([x[:, start : start + width] for x in phases[name].parts], core)
        far = same_order([x[:, start : start + width] for x in phases["far " + name].parts], core)
        return near + far

    low_pad = jnp.pad(w_lowrank, ((0, 0), (0, 128 - w_lowrank.shape[1])))
    hidden_width = w_gate.shape[1] // 2
    wide_mixer = 2 * KD + 2 * VD
    width = wide_mixer + 128
    fill = width - VD
    chip_mixer = own_columns([w_query, w_key, w_value, w_outgate], [low_pad])
    phases["mixer"] = Spread(chip_mixer)
    phases["far mixer"] = Spread(swap(chip_mixer, "dp"))
    plane.slot()
    tokens, cotangent, w_output, w_gate = tie((tokens, cotangent, w_output, w_gate), chip_mixer)
    chip_gate = own_columns([w_gate])
    chip_two = jnp.concatenate([own_columns([w_output.T]), chip_gate[:, :fill]], 1)
    phases["two"] = Spread(chip_two)
    plane.slot()
    w_up, w_down = tie((w_up, w_down), plane.done[0])
    chip_three = jnp.concatenate([chip_gate[:, fill:], own_columns([w_up])], 1)
    chip_down = own_columns([w_down.T])
    phases["three"] = Spread(chip_three)
    phases["down"] = Spread(chip_down)
    rows = chip_two.shape[0]
    far_both = jnp.concatenate([chip_two, chip_three], 0)
    far_both = swap(far_both, "dp")
    phases["far two"] = Spread(far_both[:rows])
    phases["far three"] = Spread(far_both[rows:])
    phases["far down"] = Spread(swap(tie(chip_down, phases["far mixer"].parts[0]), "dp"))
    plane.until("mixer", "far mixer")
    w_mixer = jnp.concatenate(gathered("mixer", 0, width), 0)

    cot, low_tokens = reorder(place_of, cotangent, tokens)
    gains = jnp.concatenate([mix_gain[None], mlp_gain[None]], 0)
    gains = reorder(place_of, jnp.pad(gains, ((0, 6), (0, 0))))[0]
    gain1, gain2 = gains[0], gains[1]
    cot_both = both(cot, core)
    inputs = low_tokens.astype(F32)
    length = 2 * tokens.shape[0]

    normed, norm_back = jax.vjp(rms_norm, inputs, gain1)
    normed_own = normed.astype(BF16)
    normed_low = both(normed_own, core)
    projected = matmul(normed_low, w_mixer)
    outgate = projected[:, 2 * KD + VD : wide_mixer]
    rank = w_lowrank.shape[1]
    rank_part = projected[:, wide_mixer : wide_mixer + rank].astype(BF16)
    rate = jnp.where(core == 0, w_rate[:, :KD], w_rate[:, KD:])
    bias = jnp.where(core == 0, rate_bias[:KD], rate_bias[KD:])
    logit = matmul(rank_part, rate) + bias
    decay = jax.nn.log_sigmoid(logit) / normalizer
    local_output, lifted, states, state_end, edge, fades = mixer_forward(projected, decay)
    incoming_state = incoming(edge, state_end)
    mixed_output = local_output + dot(lifted, incoming_state, (1, 1), PASSES)
    plane.until("two")
    while len(plane.done) < 9:
        plane.slot()
    plane.slot(incoming_state)
    plane.until("far two")
    w_out = jnp.concatenate(gathered("two", 0, VD), 0)
    gated, gated_back = jax.vjp(head_norm, mixed_output, outgate, head_gain)
    gated_low = gated.astype(BF16)
    mixer_chip = core_sum(times_back(gated_low, w_out), core)
    mixer_head = swap(mixer_chip, "head")
    plane.slot(mixer_chip)
    plane.slot(mixer_head)
    plane.until(*phases)
    middle = inputs + (mixer_chip.astype(F32) + mixer_head.astype(F32))
    rest = hidden_width - fill
    full_gate = jnp.concatenate(
        [
            jnp.concatenate(pair, 1)
            for pair in zip(gathered("two", VD, fill), gathered("three", 0, rest))
        ],
        0,
    )
    full_up = jnp.concatenate(gathered("three", rest, hidden_width), 0)
    w_dn = jnp.concatenate(gathered("down", 0, hidden_width), 0)
    normed2, norm2_back = jax.vjp(rms_norm, middle, gain2)
    normed2_low = both(normed2.astype(BF16), core)
    gate = matmul(normed2_low, full_gate)
    upward = matmul(normed2_low, full_up)
    hidden_low = swiglu(gate, upward).astype(BF16)
    cot_core = core_order(cot_both, core)
    normed_core = core_order(normed_low, core)
    normed2_core = core_order(normed2_low, core)
    back = Plane(
        [
            [("far down", 0)],
            [("down", 0)],
            [("far gate", 0), ("far down", 1)],
            [("gate", 0), ("down", 1)],
            [("far up", 0), ("far gate", 1)],
            [("up", 0), ("gate", 1)],
            [("far output", 0), ("far up", 1)],
            [("output", 0), ("up", 1)],
            [("far qkv", 0), ("far output", 1)],
            [("qkv", 0), ("output", 1)],
            [("far qkv", 1)],
            [("qkv", 1)],
        ],
        reverse=True,
    )
    sums = back.phases
    sums["far down"], sums["down"] = halves([(cot_core, hidden_low)])
    back.slot(plane.done[-1])
    back.slot()

    gate, upward, full_gate, full_up = tie((gate, upward, full_gate, full_up), w_dn)
    grad_hidden = matmul(cot_both, w_dn)
    sigma = jax.nn.sigmoid(gate)
    gate_low = (grad_hidden * upward * sigma * (1.0 + gate * (1.0 - sigma))).astype(BF16)
    upward_low = (grad_hidden * gate * sigma).astype(BF16)
    part = times_back(gate_low, full_gate) + times_back(upward_low, full_up)
    chip_sum = core_sum(part, core)
    head_part = swap(chip_sum, "head")
    grad_normed2 = chip_sum.astype(F32) + head_part.astype(F32)
    sums["far gate"], sums["gate"] = halves([(normed2_core, gate_low)])
    sums["far up"], sums["up"] = halves([(normed2_core, upward_low)])
    back.slot()
    back.slot()
    feed_chip = core_sum(times_back(tie(hidden_low, chip_sum), w_dn), core)
    feed_head = swap(tie(feed_chip, head_part), "head")
    result = reorder(back_place, (middle + (feed_chip.astype(F32) + feed_head.astype(F32))).astype(BF16))[0]
    back.slot(chip_sum)
    back.slot(feed_chip)
    middle_grad, grad_mlp_gain = norm2_back(grad_normed2)
    grad_middle = cot.astype(F32) + middle_grad
    middle_low = both(grad_middle.astype(BF16), core)
    grad_gated = matmul(middle_low, w_out)
    mixed_gradient, outgate_grad, head_gain_part = gated_back(grad_gated)
    outgate_low = outgate_grad.astype(BF16)
    middle_core = core_order(middle_low, core)
    sums["far output"], sums["output"] = halves(
        [(middle_core, gated_low), (normed_core, outgate_low)]
    )
    outgoing = incoming(edge, dot(mixed_gradient, lifted, (0, 0), PASSES), reverse=True)
    if len(chip_bits()) == 2:
        back.slot()
        back.slot(outgoing, feed_head)
    qkv_low, decay_grad = mixer_backward(
        projected, decay, mixed_gradient, states, fades, incoming_state, outgoing
    )
    logit_low = (decay_grad * jax.nn.sigmoid(-logit) / normalizer).astype(BF16)
    grad_rate = inner(rank_part, logit_low)
    grad_rate_bias = jnp.sum(logit_low.astype(F32), axis=0)
    rank_low = times_back(logit_low, rate).astype(BF16)
    rank_low = jnp.pad(rank_low, ((0, 0), (0, 128 - rank)))
    mixer_low = jnp.concatenate([qkv_low, outgate_low, rank_low], 1)
    normed_chip = core_sum(times_back(mixer_low, w_mixer), core)
    normed_head = swap(normed_chip, "head")
    grad_normed = normed_chip.astype(F32) + normed_head.astype(F32)
    qkv_rank = jnp.concatenate([qkv_low, rank_low], 1)
    sums["far qkv"], sums["qkv"] = halves([(normed_core, qkv_rank)])
    back.slot(normed_chip)
    back.slot()
    back.slot(result)
    back.slot(normed_head)
    back.until(*sums)
    inputs_grad, grad_mix_gain = norm_back(grad_normed)
    grad_tokens = reorder(back_place, grad_middle + inputs_grad)[0]

    finished = []
    for i, name in enumerate(("down", "gate", "up", "output", "qkv")):
        got = swap(sums["far " + name].rows.astype(BF16), "dp")
        if 2 * i + 4 < len(back.done):
            got = tie(got, back.done[2 * i + 4])
        finished.append(sums[name].rows + got.astype(F32))
    grad_down, grad_gate, grad_up, grad_output, grad_qkv = finished

    def own_rows(chip_rows):
        mine = jnp.where(core == 0, chip_rows[:wide], chip_rows[wide:])
        theirs = jnp.where(core == 0, chip_rows[wide:], chip_rows[:wide])
        got = swap(theirs.astype(BF16), "seq", CORE).astype(F32)
        return jnp.where(core == 0, mine, got), jnp.where(core == 0, got, mine)

    def columns(pair, start, width):
        return jnp.concatenate([part[:, start : start + width] for part in pair], 1)

    qkv_pair = own_rows(grad_qkv[:, : 2 * KD + VD])
    sum_query = columns(qkv_pair, 0, KD)
    sum_key = columns(qkv_pair, KD, KD)
    sum_value = columns(qkv_pair, 2 * KD, VD)
    low_rows = grad_qkv[:, 2 * KD + VD : 2 * KD + VD + rank]
    low_mine = jnp.where(core == 0, low_rows[:wide], low_rows[wide:])
    low_theirs = jnp.where(core == 0, low_rows[wide:], low_rows[:wide])
    low_mine = low_mine + swap(low_theirs, "seq", CORE)
    sum_lowrank = low_mine + swap(low_mine, "head")
    output_pair = own_rows(grad_output)
    sum_output = columns(output_pair, 0, VD).T
    sum_outgate = columns(output_pair, VD, VD)
    sum_gate = jnp.concatenate(own_rows(grad_gate), 1)
    sum_up = jnp.concatenate(own_rows(grad_up), 1)
    sum_down = jnp.concatenate(own_rows(grad_down), 1).T

    zero = jnp.zeros_like(grad_rate)
    wide_rate = jnp.where(
        core == 0,
        jnp.concatenate([grad_rate, zero], 1),
        jnp.concatenate([zero, grad_rate], 1),
    )
    wide_bias = jnp.where(
        core == 0,
        jnp.concatenate([grad_rate_bias, zero[0]]),
        jnp.concatenate([zero[0], grad_rate_bias]),
    )
    head_gain_part = head_gain_part + swap(head_gain_part[None], "head")[0]
    gains = jnp.pad(jnp.stack([grad_mix_gain, grad_mlp_gain]), ((0, 6), (0, 0)))
    gains = reorder(back_place, gains)[0][:2]
    model = gains.shape[1]
    others = jnp.concatenate([wide_rate.reshape(-1), wide_bias, head_gain_part])
    others = jnp.pad(others, (0, 6 * model - others.shape[0])).reshape(6, model)
    small = jnp.concatenate([gains, others], 0)
    for axis, bits in (("seq", [CORE] + chip_bits()), ("dp", [1])):
        for bit in bits:
            small = small + swap(small, axis, bit)
    sum_mix_gain, sum_mlp_gain = small[0], small[1]
    others = small[2:].reshape(-1)
    at = wide_rate.size
    sum_rate = others[:at].reshape(wide_rate.shape)
    sum_rate_bias = others[at : at + wide_bias.size]
    at = at + wide_bias.size
    sum_head_gain = others[at : at + VD]
    return (
        result,
        grad_tokens,
        sum_mix_gain,
        sum_query,
        sum_key,
        sum_value,
        sum_outgate,
        sum_lowrank,
        sum_rate,
        sum_rate_bias,
        sum_head_gain,
        sum_output,
        sum_mlp_gain,
        sum_gate,
        sum_up,
        sum_down,
    )


def solution(mesh):
    rows = P(("dp", "seq"), None)
    in_columns = P(("dp", "seq"), "head")
    in_rows = P("head", ("dp", "seq"))
    in_specs = (
        rows,
        P(),
        in_columns,
        in_columns,
        in_columns,
        in_columns,
        rows,
        P(None, "head"),
        P("head"),
        P(),
        in_rows,
        P(),
        in_columns,
        in_columns,
        in_rows,
        rows,
    )
    out_specs = (
        rows,
        rows,
        P(),
        in_columns,
        in_columns,
        in_columns,
        in_columns,
        rows,
        P(None, "head"),
        P("head"),
        P(),
        in_rows,
        P(),
        in_columns,
        in_columns,
        in_rows,
    )
    return jax.shard_map(body, mesh=mesh, in_specs=in_specs, out_specs=out_specs, check_vma=False)
```

```python
import functools

import jax
import jax.numpy as jnp
from jax import lax
from jax.experimental import pallas as pl
from jax.experimental.pallas import tpu as pltpu
from jax.sharding import PartitionSpec as P

KD = 256
VD = 512
BLOCK_LEN = 64

epsilon = 1e-06
normalizer = 16.0
MATMUL_PRECISION = lax.Precision.HIGHEST
BF16 = jnp.bfloat16
F32 = jnp.float32
CORE = 1


ORDER = {'rest': [], 'lag': 0, 'early': 0, 'pieces a': 1, 'pieces b': 1, 'pieces c': 1, 'far two': [], 'one': ['zero', 'far mixer'], 'far three': ['one', 'far two'], 'two': ['one', 'far two'], 'projected': [], 'far down': ['two', 'far three', 'state'], 'three': ['two', 'far three', 'state'], 'mixed': [], 'four': ['three', 'far down', 'incoming'], 'five': ['four', 'chip'], 'gate': ['four'], 'b0': ['five'], 'b1': [], 'hidden': [], 'G dots': [], 'part gate': ['G', 'b0'], 'part up': ['G', 'b1'], 'U dots': ['chip2'], 'b2': [], 'b3': ['chip2'], 'feed': ['U', 'b2'], 'b4': ['head2'], 'feed head': ['head2'], 'norm2': [], 'gated': [], 'b5': ['feed'], 'dp D': ['head2'], 'dp G': [], 'O dots': ['contribution', 'D sum'], 'b6': ['outgoing'], 'kernel': ['O', 'b5', 'G sum'], 'normed': ['b5'], 'Q dots': ['chip3'], 'result': ['qkv'], 'b7': ['chip3'], 'b8': [], 'b9': [], 'b10': ['head3'], 'b11': ['head3'], 'dp Q': ['head3'], 'dp U': [], 'dp O': [], 'tail': ['b11', 'b9'], 'end down': ['chip3'], 'end gate': ['qkv'], 'end up': ['b9'], 'end output': [], 'end qkv': [], 'cost f': 0, 'cost b': 0}


def swap(x, axis, bit=1):
    count = lax.axis_size(axis)
    return lax.ppermute(x, axis, [(i, i ^ bit) for i in range(count)])


def matmul(left, right):
    return jnp.dot(left, right, preferred_element_type=F32)


def inner(left, right):
    return lax.dot_general(left, right, (((0,), (0,)), ((), ())), preferred_element_type=F32)


def times_back(grad, weight):
    return lax.dot_general(grad, weight, (((1,), (1,)), ((), ())), preferred_element_type=F32)


def rms_norm(x, gain):
    return x * lax.rsqrt(jnp.mean(x * x, axis=-1, keepdims=True) + epsilon) * gain


def head_norm(mixed_output, outgate, gain):
    return rms_norm(mixed_output, gain) * jax.nn.silu(outgate)


def swiglu(gate, upward):
    return jax.nn.silu(gate) * upward


def dot(a, b, contract, passes=1):
    dims = ((contract[0],), (contract[1],)), ((), ())

    def once(x, y):
        return lax.dot_general(x, y, dims, preferred_element_type=F32)

    high_a, high_b = a.astype(BF16), b.astype(BF16)
    total = once(high_a, high_b)
    if passes > 1:
        low_a = (a - high_a.astype(F32)).astype(BF16)
        low_b = (b - high_b.astype(F32)).astype(BF16)
        total = total + (once(high_a, low_b) + once(low_a, high_b))
    return total


def triangle(size):
    rows = lax.broadcasted_iota(jnp.int32, (size, size), 0)
    columns = lax.broadcasted_iota(jnp.int32, (size, size), 1)
    return rows >= columns


def block_terms(query, key, decay):
    size = decay.shape[0]
    ones = jnp.where(triangle(size), 1.0, 0.0)
    running = lax.dot_general(
        ones, decay, (((1,), (0,)), ((), ())), precision=MATMUL_PRECISION, preferred_element_type=F32
    )
    final = running[size - 1 : size]
    rise, fall, rest = jnp.exp(running), jnp.exp(-running), jnp.exp(final - running)
    return query * (KD**-0.5) * rise, key * fall, key * rest, rise, fall, rest, final


PASSES = 1


def forward_kernel(q_ref, k_ref, v_ref, d_ref, out_ref, lifted_ref, states_ref, end_ref, edge_ref, prefix_ref, state, before):
    @pl.when(pl.program_id(0) == 0)
    def _():
        state[...] = jnp.zeros_like(state)
        before[...] = jnp.zeros_like(before)

    lifted, lowered, carried, _, _, _, final = block_terms(q_ref[...], k_ref[...], d_ref[...])
    value = v_ref[...]
    scores = dot(lifted, lowered, (1, 1), PASSES)
    scores = jnp.where(triangle(scores.shape[0]), scores, 0.0)
    held = state[...]
    out_ref[...] = dot(scores, value, (1, 0), PASSES) + dot(lifted, held, (1, 1), PASSES)
    reach = jnp.exp(before[0:1])
    lifted_ref[...] = lifted * reach
    prefix_ref[...] = reach[None]
    states_ref[...] = held[None]
    new = held * jnp.exp(final) + dot(value, carried, (0, 0), PASSES)
    state[...] = new
    before[0:1] = before[0:1] + final
    end_ref[...] = new
    edge_ref[...] = jnp.exp(before[0:1])


def backward_kernel(q_ref, k_ref, v_ref, d_ref, grad_ref, states_ref, prefix_ref, in_ref, out_ref, mixer_ref, decay_ref, state):
    @pl.when(pl.program_id(0) == 0)
    def _():
        state[...] = out_ref[...]

    lifted, lowered, carried, rise, fall, rest, final = block_terms(q_ref[...], k_ref[...], d_ref[...])
    value, grad = v_ref[...], grad_ref[...]
    later = state[...]
    held = states_ref[0] + in_ref[...] * prefix_ref[0]
    lower = triangle(value.shape[0])
    scores = jnp.where(lower, dot(lifted, lowered, (1, 1), PASSES), 0.0)
    grad_scores = jnp.where(lower, dot(grad, value, (1, 1), PASSES), 0.0)
    grad_value = dot(scores, grad, (0, 0), PASSES) + dot(carried, later, (1, 1), PASSES)
    grad_lifted = dot(grad, held, (1, 0), PASSES) + dot(grad_scores, lowered, (1, 0), PASSES)
    grad_lowered = dot(grad_scores, lifted, (0, 0), PASSES)
    grad_carried = dot(value, later, (1, 0), PASSES)
    mixer_ref[:, :KD] = (grad_lifted * rise * (KD**-0.5)).astype(BF16)
    mixer_ref[:, KD : 2 * KD] = (grad_lowered * fall + grad_carried * rest).astype(BF16)
    mixer_ref[:, 2 * KD :] = grad_value.astype(BF16)
    through = carried * grad_carried
    change = lifted * grad_lifted - lowered * grad_lowered - through
    fade = jnp.exp(final)
    last = jnp.sum(through, axis=0, keepdims=True) + fade * jnp.sum(held * later, axis=0, keepdims=True)
    ones = jnp.where(lower, 1.0, 0.0)
    decay_ref[...] = last + lax.dot_general(
        ones, change, (((0,), (0,)), ((), ())), precision=MATMUL_PRECISION, preferred_element_type=F32
    )
    state[...] = later * fade + dot(grad, lifted, (0, 0), PASSES)


def cost(key):
    flops = (None, 10**6, 2 * 10**10)[ORDER[key]]
    if flops is None:
        return None
    return pl.CostEstimate(flops=flops, bytes_accessed=10**5, transcendentals=0)


def mixer_forward(projected, decay):
    length = decay.shape[0]
    count = length // BLOCK_LEN
    row = lambda i: (i, 0)
    fixed = lambda i: (0, 0)
    return pl.pallas_call(
        forward_kernel,
        grid=(count,),
        in_specs=[
            pl.BlockSpec((BLOCK_LEN, KD), lambda i: (i, 0)),
            pl.BlockSpec((BLOCK_LEN, KD), lambda i: (i, 1)),
            pl.BlockSpec((BLOCK_LEN, VD), lambda i: (i, 1)),
            pl.BlockSpec((BLOCK_LEN, KD), row),
        ],
        out_specs=[
            pl.BlockSpec((BLOCK_LEN, VD), row),
            pl.BlockSpec((BLOCK_LEN, KD), row),
            pl.BlockSpec((1, VD, KD), lambda i: (i, 0, 0)),
            pl.BlockSpec((VD, KD), fixed),
            pl.BlockSpec((1, KD), fixed),
            pl.BlockSpec((1, 1, KD), lambda i: (i, 0, 0)),
        ],
        out_shape=[
            jax.ShapeDtypeStruct((length, VD), F32),
            jax.ShapeDtypeStruct((length, KD), F32),
            jax.ShapeDtypeStruct((count, VD, KD), F32),
            jax.ShapeDtypeStruct((VD, KD), F32),
            jax.ShapeDtypeStruct((1, KD), F32),
            jax.ShapeDtypeStruct((count, 1, KD), F32),
        ],
        scratch_shapes=[pltpu.VMEM((VD, KD), F32), pltpu.VMEM((8, KD), F32)],
        compiler_params=pltpu.CompilerParams(
            dimension_semantics=("arbitrary",), vmem_limit_bytes=32 * 2**20
        ),
        cost_estimate=cost("cost f"),
        name="mixer_forward",
    )(projected, projected, projected, decay)


def mixer_backward(projected, decay, grad, states, prefix, earlier, later):
    length = decay.shape[0]
    count = length // BLOCK_LEN
    row = lambda i: (count - 1 - i, 0)
    fixed = lambda i: (0, 0)
    return pl.pallas_call(
        backward_kernel,
        grid=(count,),
        in_specs=[
            pl.BlockSpec((BLOCK_LEN, KD), lambda i: (count - 1 - i, 0)),
            pl.BlockSpec((BLOCK_LEN, KD), lambda i: (count - 1 - i, 1)),
            pl.BlockSpec((BLOCK_LEN, VD), lambda i: (count - 1 - i, 1)),
            pl.BlockSpec((BLOCK_LEN, KD), row),
            pl.BlockSpec((BLOCK_LEN, VD), row),
            pl.BlockSpec((1, VD, KD), lambda i: (count - 1 - i, 0, 0)),
            pl.BlockSpec((1, 1, KD), lambda i: (count - 1 - i, 0, 0)),
            pl.BlockSpec((VD, KD), fixed),
            pl.BlockSpec((VD, KD), fixed),
        ],
        out_specs=[
            pl.BlockSpec((BLOCK_LEN, 2 * KD + VD), row),
            pl.BlockSpec((BLOCK_LEN, KD), row),
        ],
        out_shape=[
            jax.ShapeDtypeStruct((length, 2 * KD + VD), BF16),
            jax.ShapeDtypeStruct((length, KD), F32),
        ],
        scratch_shapes=[pltpu.VMEM((VD, KD), F32)],
        compiler_params=pltpu.CompilerParams(
            dimension_semantics=("arbitrary",), vmem_limit_bytes=32 * 2**20
        ),
        cost_estimate=cost("cost b"),
        name="mixer_backward",
    )(projected, projected, projected, decay, grad, states, prefix, earlier, later)


def chip_bits():
    bits, bit = [], 2
    while bit < lax.axis_size("seq"):
        bits.append(bit)
        bit *= 2
    return bits


def tie(arrays, *first):
    return lax.optimization_barrier((arrays, first))[0]


def hop(x, step):
    bits = chip_bits()
    there = (bits[step], bits[-1 - step])
    count = lax.axis_size("seq")
    return lax.ppermute(x, "seq", [(i, i ^ there[i % 2]) for i in range(count)])


def place_in(core_order):
    count = len(chip_bits())
    return sum(((core_order >> k) & 1) << (count - 1 - k) for k in range(count))


def same_order(parts, core):
    return [
        x if place_in(i) == i else jnp.where(core == 0, x, parts[place_in(i)])
        for i, x in enumerate(parts)
    ]


class Spread:
    def __init__(self, rows):
        self.parts = [rows]
        self.steps = 0

    def load(self):
        return self.parts[0] if len(self.parts) == 1 else jnp.concatenate(self.parts, 0)

    def take(self, got):
        rows = self.parts[0].shape[0]
        count = len(self.parts)
        self.parts = self.parts + [got[i * rows : (i + 1) * rows] for i in range(count)]
        self.steps += 1


class Collect:
    def __init__(self, rows):
        self.rows = rows
        self.steps = 0

    def load(self):
        return self.rows[self.rows.shape[0] // 2 :]

    def take(self, got):
        kept = self.rows[: self.rows.shape[0] // 2].astype(F32)
        self.rows = (kept + got.astype(F32)).astype(BF16)
        self.steps += 1


class Plane:
    def __init__(self, plan, reverse=False):
        names = sorted({name for slot in plan for name, _ in slot}, key=str(plan).index)
        steps = len(chip_bits())
        self.plan = plan if steps == 2 else [[(n, i)] for n in names for i in range(steps)]
        self.phases = {}
        self.reverse = reverse
        self.done = []

    def slot(self, *first):
        now = self.plan[len(self.done)]
        loads = [self.phases[name].load() for name, _ in now]
        if len(self.done) >= 2 and ORDER["lag"]:
            first = first + (self.done[-2],)
        if first:
            loads = tie(loads, *first)
        landed = []
        for (name, i), x in zip(now, loads):
            got = hop(x, len(chip_bits()) - 1 - i if self.reverse else i)
            self.phases[name].take(got)
            landed.append(got)
        self.done.append(landed)

    def until(self, *names):
        while any(self.phases[name].steps < len(chip_bits()) for name in names):
            self.slot()


def order():
    chip, dp = lax.axis_index("seq") // 2, lax.axis_index("dp")
    near = [0]
    for bit in chip_bits():
        near = near + [place ^ (bit // 2) for place in near]
    chips = len(near)
    return [(dp ^ away) * chips + (chip ^ place) for away in range(2) for place in near]


def reorder_kernel(count, index_ref, *refs):
    half = len(refs) // 2
    for source, target in zip(refs[:half], refs[half:]):
        width = source.shape[1] // count
        for i in range(count):
            start = pl.multiple_of(index_ref[i] * width, width)
            target[:, i * width : (i + 1) * width] = source[:, pl.ds(start, width)]


def reorder(index, *arrays):
    count = index.shape[0]
    rows, columns = arrays[0].shape
    if (columns // count) % 128:
        moved = [
            jnp.take(x.reshape(rows, count, -1), index, axis=1).reshape(rows, columns)
            for x in arrays
        ]
        return moved
    step = rows // 3 if rows % 48 == 0 else rows
    spec = pl.BlockSpec((step, columns), lambda i, _: (i, 0))
    return pl.pallas_call(
        functools.partial(reorder_kernel, count),
        grid_spec=pltpu.PrefetchScalarGridSpec(
            num_scalar_prefetch=1,
            grid=(rows // step,),
            in_specs=[spec] * len(arrays),
            out_specs=[spec] * len(arrays),
        ),
        out_shape=[jax.ShapeDtypeStruct(x.shape, x.dtype) for x in arrays],
        compiler_params=pltpu.CompilerParams(
            dimension_semantics=("arbitrary",), vmem_limit_bytes=32 * 2**20
        ),
        name="reorder",
    )(index, *arrays)


def core_order(x, core):
    count = 2 * 2 ** len(chip_bits())
    parts = jnp.split(x, count, 1)
    half = count // 2
    return jnp.concatenate(same_order(parts[:half], core) + same_order(parts[half:], core), 1)


def halves(pairs):
    half = pairs[0][0].shape[1] // 2

    def part(i):
        grads = [inner(left[:, i * half : (i + 1) * half], right) for left, right in pairs]
        return jnp.concatenate([grad.astype(BF16) for grad in grads], 1)

    return Collect(part(1)), Collect(part(0))


def both(x, core):
    other = swap(x, "seq", CORE)
    return jnp.concatenate([jnp.where(core == 0, x, other), jnp.where(core == 0, other, x)], 0)


def core_sum(part, core):
    rows = part.shape[0] // 2
    mine = jnp.where(core == 0, part[:rows], part[rows:])
    theirs = jnp.where(core == 0, part[rows:], part[:rows])
    mine = mine + swap(theirs.astype(BF16), "seq", CORE).astype(F32)
    return mine.astype(BF16)


def add_up(part, core):
    mine = core_sum(part, core)
    return mine.astype(F32) + swap(mine, "head").astype(F32)


def incoming(edge, state, reverse=False):
    chips = lax.axis_size("seq") // 2
    rows = state.shape[0]
    high = edge.astype(BF16)
    low = (edge - high.astype(F32)).astype(BF16)
    edges = jnp.pad(jnp.concatenate([high, low], 0), ((0, 14), (0, 0)))
    packed = jnp.concatenate([state.astype(BF16), edges], 0)

    def move(by):
        by = -by if reverse else by
        pairs = []
        for i in range(chips):
            if 0 <= i + by < chips:
                for c in range(2):
                    pairs.append((2 * i + c, 2 * (i + by) + c))
        return lax.ppermute(packed, "seq", pairs).astype(F32)

    total, faded = jnp.zeros_like(state), None
    for by in range(1, chips):
        there = move(by)
        gone = there[rows : rows + 1] + there[rows + 1 : rows + 2]
        if by == 1:
            total, faded = there[:rows], gone
        else:
            total, faded = total + faded * there[:rows], faded * gone
    return total


def body(
    tokens,
    mix_gain,
    w_query,
    w_key,
    w_value,
    w_outgate,
    w_lowrank,
    w_rate,
    rate_bias,
    head_gain,
    w_output,
    mlp_gain,
    w_gate,
    w_up,
    w_down,
    cotangent,
):
    core = lax.axis_index("seq") % 2
    blocks = order()
    wide = tokens.shape[1] // (2 * len(blocks))
    place_of = jnp.stack(blocks).astype(jnp.int32)
    places = jnp.arange(len(blocks), dtype=jnp.int32)
    back_place = jnp.sum(
        jnp.where(place_of[None] == places[:, None], places[None], 0), axis=1, dtype=jnp.int32
    )

    def split(w):
        half = w.shape[1] // 2
        mine = jnp.where(core == 0, w[:, :half], w[:, half:])
        theirs = jnp.where(core == 0, w[:, half:], w[:, :half])
        return mine, theirs

    def own_columns(weights, shared=()):
        pairs = [split(w) for w in weights] + [(w, w) for w in shared]
        mine = jnp.concatenate([p[0] for p in pairs], 1)
        got = swap(jnp.concatenate([p[1] for p in pairs], 1), "seq", CORE)
        return jnp.concatenate(
            [jnp.where(core == 0, mine, got), jnp.where(core == 0, got, mine)], 0
        )

    bits = len(chip_bits())
    phases = {}
    seen = {}

    def after(x, key):
        first = [seen[name] for name in ORDER[key] if name in seen]
        return tie(x, *first) if first else x

    def exchange(x, key):
        count = ORDER[key]
        size = x.shape[0] // count
        parts = [swap(x[i * size : (i + 1) * size], "head") for i in range(count)]
        for i, part in enumerate(parts):
            seen[key + str(i)] = part
        return jnp.concatenate(parts, 0) if count > 1 else parts[0]

    def slot(hops, key):
        loads = after([phases[name].load() for name in hops], key)
        landed = []
        for name, x in zip(hops, loads):
            got = hop(x, phases[name].steps)
            phases[name].take(got)
            landed.append(got)
        return landed

    def rest_of(*names):
        for name in names:
            while phases[name].steps < bits:
                slot([name], "rest")

    def gathered(name, start, width):
        near = same_order([x[:, start : start + width] for x in phases[name].parts], core)
        far = same_order([x[:, start : start + width] for x in phases["far " + name].parts], core)
        return near + far

    low_pad = jnp.pad(w_lowrank, ((0, 0), (0, 128 - w_lowrank.shape[1])))
    hidden_width = w_gate.shape[1] // 2
    wide_mixer = 2 * KD + 2 * VD
    width = wide_mixer + 128
    fill = width - VD
    chip_mixer = own_columns([w_query, w_key, w_value, w_outgate], [low_pad])
    phases["mixer"] = Spread(chip_mixer)
    far_mixer = swap(chip_mixer, "dp")
    zero = slot(["mixer"], "rest")
    w_output, w_gate, w_up, w_down = tie((w_output, w_gate, w_up, w_down), chip_mixer)
    chip_gate = own_columns([w_gate])
    chip_two = jnp.concatenate([own_columns([w_output.T]), chip_gate[:, :fill]], 1)
    chip_three = jnp.concatenate([chip_gate[:, fill:], own_columns([w_up])], 1)
    chip_down = own_columns([w_down.T])
    phases["two"], phases["three"] = Spread(chip_two), Spread(chip_three)
    phases["down"] = Spread(chip_down)
    zero += slot(["two", "three", "down"], "rest")
    seen["zero"], seen["far mixer"] = zero, far_mixer
    tokens, cotangent = tie((tokens, cotangent), chip_down)
    phases["far mixer"] = Spread(far_mixer)
    far_two = swap(after(chip_two, "far two"), "dp")
    seen["one"] = slot(["far mixer", "mixer", "two"], "one")
    rest_of("mixer", "two")
    seen["far two"] = far_two
    phases["far two"] = Spread(far_two)
    far_three = swap(after(chip_three, "far three"), "dp")
    seen["two"] = slot(["far mixer", "far two", "three"], "two")
    rest_of("far mixer", "three")
    if bits > 2:
        rest_of("far two")
    seen["far three"] = far_three
    phases["far three"] = Spread(far_three)
    w_mixer = jnp.concatenate(gathered("mixer", 0, width), 0)

    cot, low_tokens = reorder(place_of, cotangent, tokens)
    gains = jnp.concatenate([mix_gain[None], mlp_gain[None]], 0)
    gains = reorder(place_of, jnp.pad(gains, ((0, 6), (0, 0))))[0]
    gain1, gain2 = gains[0], gains[1]
    cot_both = both(cot, core)
    inputs = low_tokens.astype(F32)
    length = 2 * tokens.shape[0]

    normed, norm_back = jax.vjp(rms_norm, inputs, gain1)
    normed_own = normed.astype(BF16)
    normed_low = both(normed_own, core)
    projected = matmul(after(normed_low, "projected"), w_mixer)
    outgate = projected[:, 2 * KD + VD : wide_mixer]
    rank = w_lowrank.shape[1]
    rank_part = projected[:, wide_mixer : wide_mixer + rank].astype(BF16)
    rate = jnp.where(core == 0, w_rate[:, :KD], w_rate[:, KD:])
    bias = jnp.where(core == 0, rate_bias[:KD], rate_bias[KD:])
    logit = matmul(rank_part, rate) + bias
    decay = jax.nn.log_sigmoid(logit) / normalizer
    local_output, lifted, states, state_end, edge, fades = mixer_forward(projected, decay)
    seen["state"] = state_end
    far_down = swap(after(chip_down, "far down"), "dp")
    seen["three"] = slot(
        (["far two", "far three"] if bits == 2 else ["far three"]) + ["down"] * ORDER["early"], "three"
    )
    rest_of("far two")
    phases["far down"] = Spread(far_down)
    incoming_state = incoming(edge, state_end)
    seen["incoming"] = incoming_state
    mixed_output = local_output + dot(lifted, after(incoming_state, "mixed"), (1, 1), PASSES)
    seen["far down"] = far_down
    seen["four"] = slot(["far three"] + ["down"] * (1 - ORDER["early"]) + ["far down"], "four")
    rest_of("far three", "down")
    w_out = jnp.concatenate(gathered("two", 0, VD), 0)
    gated, gated_back = jax.vjp(head_norm, mixed_output, outgate, head_gain)
    gated_low = gated.astype(BF16)
    mixer_chip = core_sum(times_back(gated_low, w_out), core)
    seen["chip"] = mixer_chip
    mixer_head = exchange(mixer_chip, "pieces a")
    seen["head"] = mixer_head
    seen["five"] = slot(["far down"], "five")
    rest_of("far down")
    middle = inputs + (mixer_chip.astype(F32) + mixer_head.astype(F32))
    rest = hidden_width - fill
    full_gate = jnp.concatenate(
        [
            jnp.concatenate(pair, 1)
            for pair in zip(gathered("two", VD, fill), gathered("three", 0, rest))
        ],
        0,
    )
    full_up = jnp.concatenate(gathered("three", rest, hidden_width), 0)
    w_dn = jnp.concatenate(gathered("down", 0, hidden_width), 0)
    normed2, norm2_back = jax.vjp(rms_norm, middle, gain2)
    normed2_low = both(normed2.astype(BF16), core)
    normed2_low = after(normed2_low, "gate")
    gate = matmul(normed2_low, full_gate)
    upward = matmul(normed2_low, full_up)
    hidden_low = swiglu(gate, upward).astype(BF16)
    cot_core = core_order(cot_both, core)
    normed_core = core_order(normed_low, core)
    normed2_core = core_order(normed2_low, core)
    back = Plane(
        [
            [("far down", 0)],
            [("down", 0)],
            [("far gate", 0), ("far down", 1)],
            [("gate", 0), ("down", 1)],
            [("far up", 0), ("far gate", 1)],
            [("up", 0), ("gate", 1)],
            [("far output", 0), ("far up", 1)],
            [("output", 0), ("up", 1)],
            [("far qkv", 0), ("far output", 1)],
            [("qkv", 0), ("output", 1)],
            [("far qkv", 1)],
            [("qkv", 1)],
        ],
        reverse=True,
    )
    sums = back.phases
    sums["far down"], sums["down"] = halves([(cot_core, hidden_low)])
    down_rows = sums["far down"].rows, sums["down"].rows
    seen["D"] = down_rows

    def go(key):
        first = [seen[name] for name in ORDER[key] if name in seen]
        back.slot(*first)
        seen[key] = back.done[-1]

    def far_sum(name, key):
        return swap(after(sums["far " + name].rows.astype(BF16), key), "dp")

    go("b0")
    go("b1")
    grad_result, gate, upward, full_gate, full_up = after(
        tie((cot_both, gate, upward, full_gate, full_up), w_dn, down_rows), "hidden"
    )
    grad_hidden = matmul(grad_result, w_dn)
    sigma = jax.nn.sigmoid(gate)
    gate_low = (grad_hidden * upward * sigma * (1.0 + gate * (1.0 - sigma))).astype(BF16)
    upward_low = (grad_hidden * gate * sigma).astype(BF16)
    sums["far gate"], sums["gate"] = halves([(normed2_core, after(gate_low, "G dots"))])
    seen["G"] = sums["far gate"].rows, sums["gate"].rows
    part = times_back(after(gate_low, "part gate"), full_gate) + times_back(
        after(upward_low, "part up"), full_up
    )
    chip_sum = core_sum(part, core)
    seen["chip2"] = chip_sum
    head_part = exchange(chip_sum, "pieces b")
    seen["head2"] = head_part
    sums["far up"], sums["up"] = halves([(normed2_core, after(upward_low, "U dots"))])
    seen["U"] = sums["far up"].rows, sums["up"].rows
    go("b2")
    go("b3")
    feed_chip = core_sum(times_back(after(hidden_low, "feed"), w_dn), core)
    seen["feed"] = feed_chip
    go("b4")
    feed_head = swap(after(feed_chip, "feed head"), "head")
    grad_normed2 = chip_sum.astype(F32) + after(head_part, "norm2").astype(F32)
    middle_grad, grad_mlp_gain = norm2_back(grad_normed2)
    grad_middle = cot.astype(F32) + middle_grad
    middle_low = both(grad_middle.astype(BF16), core)
    seen["middle"] = middle_low
    grad_gated = matmul(after(middle_low, "gated"), w_out)
    mixed_gradient, outgate_grad, head_gain_part = gated_back(grad_gated)
    outgate_low = outgate_grad.astype(BF16)
    middle_core = core_order(middle_low, core)
    contribution = dot(mixed_gradient, lifted, (0, 0), PASSES)
    seen["contribution"] = contribution
    go("b5")
    outgoing = incoming(edge, contribution, reverse=True)
    seen["outgoing"] = outgoing
    far_sums = {}
    if bits == 2:
        far_sums["down"], far_sums["gate"] = far_sum("down", "dp D"), far_sum("gate", "dp G")
        seen["D sum"], seen["G sum"] = far_sums["down"], far_sums["gate"]
    outgate_late = after(outgate_low, "O dots")
    sums["far output"], sums["output"] = halves(
        [(middle_core, gated_low), (normed_core, outgate_late)]
    )
    seen["O"] = sums["far output"].rows, sums["output"].rows
    if bits == 2:
        go("b6")
    outgoing = after(outgoing, "kernel")
    qkv_low, decay_grad = mixer_backward(
        projected, decay, mixed_gradient, states, fades, incoming_state, outgoing
    )
    logit_low = (decay_grad * jax.nn.sigmoid(-logit) / normalizer).astype(BF16)
    grad_rate = inner(rank_part, logit_low)
    grad_rate_bias = jnp.sum(logit_low.astype(F32), axis=0)
    rank_low = times_back(logit_low, rate).astype(BF16)
    rank_low = jnp.pad(rank_low, ((0, 0), (0, 128 - rank)))
    mixer_low = jnp.concatenate([qkv_low, outgate_low, rank_low], 1)
    seen["qkv"] = qkv_low
    normed_chip = core_sum(times_back(after(mixer_low, "normed"), w_mixer), core)
    seen["chip3"] = normed_chip
    normed_head = exchange(normed_chip, "pieces c")
    seen["head3"] = normed_head
    qkv_rank = after(jnp.concatenate([qkv_low, rank_low], 1), "Q dots")
    feed_head = after(feed_head, "result")
    result = (middle + (feed_chip.astype(F32) + feed_head.astype(F32))).astype(BF16)
    result = reorder(back_place, result)[0]
    seen["result_"] = result
    sums["far qkv"], sums["qkv"] = halves([(normed_core, qkv_rank)])
    seen["Q"] = sums["far qkv"].rows, sums["qkv"].rows
    if bits == 2:
        go("b7")
    go("b8")
    go("b9")
    go("b10")
    if bits == 2:
        far_sums["qkv"] = far_sum("qkv", "dp Q")
        seen["Q sum"] = far_sums["qkv"]
    go("b11")
    back.until(*sums)
    if bits == 2:
        far_sums["up"], far_sums["output"] = far_sum("up", "dp U"), far_sum("output", "dp O")
        seen["U sum"], seen["O sum"] = far_sums["up"], far_sums["output"]
    normed_head = after(normed_head, "tail")
    grad_normed = normed_chip.astype(F32) + normed_head.astype(F32)
    inputs_grad, grad_mix_gain = norm_back(grad_normed)
    grad_tokens = reorder(back_place, grad_middle + inputs_grad)[0]

    finished = []
    for name in ("down", "gate", "up", "output", "qkv"):
        got = far_sums[name] if name in far_sums else far_sum(name, "rest")
        got = after(got, "end " + name)
        finished.append(sums[name].rows.astype(F32) + got.astype(F32))
    grad_down, grad_gate, grad_up, grad_output, grad_qkv = finished

    def own_rows(chip_rows):
        mine = jnp.where(core == 0, chip_rows[:wide], chip_rows[wide:])
        theirs = jnp.where(core == 0, chip_rows[wide:], chip_rows[:wide])
        got = swap(theirs.astype(BF16), "seq", CORE).astype(F32)
        return jnp.where(core == 0, mine, got), jnp.where(core == 0, got, mine)

    def columns(pair, start, width):
        return jnp.concatenate([part[:, start : start + width] for part in pair], 1)

    qkv_pair = own_rows(grad_qkv[:, : 2 * KD + VD])
    sum_query = columns(qkv_pair, 0, KD)
    sum_key = columns(qkv_pair, KD, KD)
    sum_value = columns(qkv_pair, 2 * KD, VD)
    low_rows = grad_qkv[:, 2 * KD + VD : 2 * KD + VD + rank]
    low_mine = jnp.where(core == 0, low_rows[:wide], low_rows[wide:])
    low_theirs = jnp.where(core == 0, low_rows[wide:], low_rows[:wide])
    low_mine = low_mine + swap(low_theirs, "seq", CORE)
    sum_lowrank = low_mine + swap(low_mine, "head")
    output_pair = own_rows(grad_output)
    sum_output = columns(output_pair, 0, VD).T
    sum_outgate = columns(output_pair, VD, VD)
    sum_gate = jnp.concatenate(own_rows(grad_gate), 1)
    sum_up = jnp.concatenate(own_rows(grad_up), 1)
    sum_down = jnp.concatenate(own_rows(grad_down), 1).T

    zero = jnp.zeros_like(grad_rate)
    wide_rate = jnp.where(
        core == 0,
        jnp.concatenate([grad_rate, zero], 1),
        jnp.concatenate([zero, grad_rate], 1),
    )
    wide_bias = jnp.where(
        core == 0,
        jnp.concatenate([grad_rate_bias, zero[0]]),
        jnp.concatenate([zero[0], grad_rate_bias]),
    )
    head_gain_part = head_gain_part + swap(head_gain_part[None], "head")[0]
    gain_rows = jnp.stack([grad_mix_gain, grad_mlp_gain])
    gain_rows = reorder(back_place, jnp.pad(gain_rows, ((0, 6), (0, 0))))[0][:2]
    model = gain_rows.shape[1]
    others = jnp.concatenate([wide_bias, head_gain_part])
    others = jnp.pad(others, (0, 2 * model - others.shape[0])).reshape(2, model)
    others = jnp.concatenate([others, wide_rate.reshape(-1, model)], 0)
    small = jnp.concatenate([gain_rows, others], 0)
    for axis, axis_bits in (("seq", [CORE] + chip_bits()), ("dp", [1])):
        for bit in axis_bits:
            small = small + swap(small, axis, bit)
    sum_mix_gain, sum_mlp_gain = small[0], small[1]
    sum_rate_bias = small[2, : wide_bias.size]
    sum_head_gain = small[2, wide_bias.size : wide_bias.size + VD]
    sum_rate = small[4:].reshape(wide_rate.shape)
    return (
        result,
        grad_tokens,
        sum_mix_gain,
        sum_query,
        sum_key,
        sum_value,
        sum_outgate,
        sum_lowrank,
        sum_rate,
        sum_rate_bias,
        sum_head_gain,
        sum_output,
        sum_mlp_gain,
        sum_gate,
        sum_up,
        sum_down,
    )


def solution(mesh):
    rows = P(("dp", "seq"), None)
    in_columns = P(("dp", "seq"), "head")
    in_rows = P("head", ("dp", "seq"))
    in_specs = (
        rows,
        P(),
        in_columns,
        in_columns,
        in_columns,
        in_columns,
        rows,
        P(None, "head"),
        P("head"),
        P(),
        in_rows,
        P(),
        in_columns,
        in_columns,
        in_rows,
        rows,
    )
    out_specs = (
        rows,
        rows,
        P(),
        in_columns,
        in_columns,
        in_columns,
        in_columns,
        rows,
        P(None, "head"),
        P("head"),
        P(),
        in_rows,
        P(),
        in_columns,
        in_columns,
        in_rows,
    )
    return jax.shard_map(body, mesh=mesh, in_specs=in_specs, out_specs=out_specs, check_vma=False)
```

```python
import functools

import jax
import jax.numpy as jnp
from jax import lax
from jax.experimental import pallas as pl
from jax.experimental.pallas import tpu as pltpu
from jax.sharding import PartitionSpec as P

KD = 256
VD = 512
BLOCK_LEN = 64

epsilon = 1e-06
normalizer = 16.0
MATMUL_PRECISION = lax.Precision.HIGHEST
BF16 = jnp.bfloat16
F32 = jnp.float32
CORE = 1


class Order:
    rest = lambda at: ()
    lag = 0
    early = 0
    pieces_a = 1
    pieces_b = 1
    pieces_c = 1
    far_two = lambda at: ()
    one = lambda at: (at.zero, at.far_mixer,)
    far_three = lambda at: (at.one, at.far_two,)
    two = lambda at: (at.one, at.far_two,)
    projected = lambda at: ()
    far_down = lambda at: (at.two, at.far_three, at.state,)
    three = lambda at: (at.two, at.far_three, at.state,)
    mixed = lambda at: ()
    four = lambda at: (at.three, at.far_down, at.incoming,)
    five = lambda at: (at.far_down,)
    gate = lambda at: (at.four,)
    b0 = lambda at: (at.five,)
    b1 = lambda at: ()
    hidden = lambda at: ()
    G_dots = lambda at: ()
    part_gate = lambda at: (at.G, at.b0,)
    part_up = lambda at: (at.G,)
    U_dots = lambda at: (at.chip2,)
    b2 = lambda at: ()
    b3 = lambda at: (at.chip2,)
    feed = lambda at: (at.U, at.b2,)
    b4 = lambda at: (at.head2,)
    feed_head = lambda at: (at.head2,)
    norm2 = lambda at: ()
    gated = lambda at: ()
    b5 = lambda at: (at.feed,)
    dp_D = lambda at: (at.head2,)
    dp_G = lambda at: ()
    O_dots = lambda at: (at.contribution, at.D_sum,)
    b6 = lambda at: (at.outgoing,)
    kernel = lambda at: (at.O, at.b5, at.G_sum,)
    normed = lambda at: (at.b5,)
    Q_dots = lambda at: (at.chip3,)
    result = lambda at: (at.qkv,)
    b7 = lambda at: (at.chip3,)
    b8 = lambda at: ()
    b9 = lambda at: ()
    b10 = lambda at: (at.head3,)
    b11 = lambda at: (at.head3,)
    dp_Q = lambda at: (at.head3,)
    dp_U = lambda at: ()
    dp_O = lambda at: ()
    tail = lambda at: (at.b11, at.b9,)
    end_down = lambda at: (at.chip3,)
    end_gate = lambda at: (at.qkv,)
    end_up = lambda at: (at.b9,)
    end_output = lambda at: ()
    end_qkv = lambda at: ()
    cost_f = 0
    cost_b = 0
    core = 1


class Seen:
    def __getattr__(self, name):
        return ()


def swap(x, axis, bit=1):
    count = lax.axis_size(axis)
    return lax.ppermute(x, axis, [(i, i ^ bit) for i in range(count)])


def matmul(left, right):
    return jnp.dot(left, right, preferred_element_type=F32)


def inner(left, right):
    return lax.dot_general(left, right, (((0,), (0,)), ((), ())), preferred_element_type=F32)


def times_back(grad, weight):
    return lax.dot_general(grad, weight, (((1,), (1,)), ((), ())), preferred_element_type=F32)


def rms_norm(x, gain):
    return x * lax.rsqrt(jnp.mean(x * x, axis=-1, keepdims=True) + epsilon) * gain


def head_norm(mixed_output, outgate, gain):
    return rms_norm(mixed_output, gain) * jax.nn.silu(outgate)


def swiglu(gate, upward):
    return jax.nn.silu(gate) * upward


def dot(a, b, contract, passes=1):
    dims = ((contract[0],), (contract[1],)), ((), ())

    def once(x, y):
        return lax.dot_general(x, y, dims, preferred_element_type=F32)

    high_a, high_b = a.astype(BF16), b.astype(BF16)
    total = once(high_a, high_b)
    if passes > 1:
        low_a = (a - high_a.astype(F32)).astype(BF16)
        low_b = (b - high_b.astype(F32)).astype(BF16)
        total = total + (once(high_a, low_b) + once(low_a, high_b))
    return total


def triangle(size):
    rows = lax.broadcasted_iota(jnp.int32, (size, size), 0)
    columns = lax.broadcasted_iota(jnp.int32, (size, size), 1)
    return rows >= columns


def block_terms(query, key, decay):
    size = decay.shape[0]
    ones = jnp.where(triangle(size), 1.0, 0.0)
    running = lax.dot_general(
        ones, decay, (((1,), (0,)), ((), ())), precision=MATMUL_PRECISION, preferred_element_type=F32
    )
    final = running[size - 1 : size]
    rise, fall, rest = jnp.exp(running), jnp.exp(-running), jnp.exp(final - running)
    return query * (KD**-0.5) * rise, key * fall, key * rest, rise, fall, rest, final


PASSES = 1


def forward_kernel(q_ref, k_ref, v_ref, d_ref, out_ref, lifted_ref, states_ref, end_ref, edge_ref, prefix_ref, state, before):
    @pl.when(pl.program_id(0) == 0)
    def _():
        state[...] = jnp.zeros_like(state)
        before[...] = jnp.zeros_like(before)

    lifted, lowered, carried, _, _, _, final = block_terms(q_ref[...], k_ref[...], d_ref[...])
    value = v_ref[...]
    scores = dot(lifted, lowered, (1, 1), PASSES)
    scores = jnp.where(triangle(scores.shape[0]), scores, 0.0)
    held = state[...]
    out_ref[...] = dot(scores, value, (1, 0), PASSES) + dot(lifted, held, (1, 1), PASSES)
    reach = jnp.exp(before[0:1])
    lifted_ref[...] = lifted * reach
    prefix_ref[...] = reach[None]
    states_ref[...] = held[None]
    new = held * jnp.exp(final) + dot(value, carried, (0, 0), PASSES)
    state[...] = new
    before[0:1] = before[0:1] + final
    end_ref[...] = new
    edge_ref[...] = jnp.exp(before[0:1])


def backward_kernel(q_ref, k_ref, v_ref, d_ref, grad_ref, states_ref, prefix_ref, in_ref, out_ref, mixer_ref, decay_ref, state):
    @pl.when(pl.program_id(0) == 0)
    def _():
        state[...] = out_ref[...]

    lifted, lowered, carried, rise, fall, rest, final = block_terms(q_ref[...], k_ref[...], d_ref[...])
    value, grad = v_ref[...], grad_ref[...]
    later = state[...]
    held = states_ref[0] + in_ref[...] * prefix_ref[0]
    lower = triangle(value.shape[0])
    scores = jnp.where(lower, dot(lifted, lowered, (1, 1), PASSES), 0.0)
    grad_scores = jnp.where(lower, dot(grad, value, (1, 1), PASSES), 0.0)
    grad_value = dot(scores, grad, (0, 0), PASSES) + dot(carried, later, (1, 1), PASSES)
    grad_lifted = dot(grad, held, (1, 0), PASSES) + dot(grad_scores, lowered, (1, 0), PASSES)
    grad_lowered = dot(grad_scores, lifted, (0, 0), PASSES)
    grad_carried = dot(value, later, (1, 0), PASSES)
    mixer_ref[:, :KD] = (grad_lifted * rise * (KD**-0.5)).astype(BF16)
    mixer_ref[:, KD : 2 * KD] = (grad_lowered * fall + grad_carried * rest).astype(BF16)
    mixer_ref[:, 2 * KD :] = grad_value.astype(BF16)
    through = carried * grad_carried
    change = lifted * grad_lifted - lowered * grad_lowered - through
    fade = jnp.exp(final)
    last = jnp.sum(through, axis=0, keepdims=True) + fade * jnp.sum(held * later, axis=0, keepdims=True)
    ones = jnp.where(lower, 1.0, 0.0)
    decay_ref[...] = last + lax.dot_general(
        ones, change, (((0,), (0,)), ((), ())), precision=MATMUL_PRECISION, preferred_element_type=F32
    )
    state[...] = later * fade + dot(grad, lifted, (0, 0), PASSES)


def cost(key):
    flops = (None, 10**6, 2 * 10**10)[key]
    if flops is None:
        return None
    return pl.CostEstimate(flops=flops, bytes_accessed=10**5, transcendentals=0)


def mixer_forward(projected, decay):
    length = decay.shape[0]
    count = length // BLOCK_LEN
    row = lambda i: (i, 0)
    fixed = lambda i: (0, 0)
    return pl.pallas_call(
        forward_kernel,
        grid=(count,),
        in_specs=[
            pl.BlockSpec((BLOCK_LEN, KD), lambda i: (i, 0)),
            pl.BlockSpec((BLOCK_LEN, KD), lambda i: (i, 1)),
            pl.BlockSpec((BLOCK_LEN, VD), lambda i: (i, 1)),
            pl.BlockSpec((BLOCK_LEN, KD), row),
        ],
        out_specs=[
            pl.BlockSpec((BLOCK_LEN, VD), row),
            pl.BlockSpec((BLOCK_LEN, KD), row),
            pl.BlockSpec((1, VD, KD), lambda i: (i, 0, 0)),
            pl.BlockSpec((VD, KD), fixed),
            pl.BlockSpec((1, KD), fixed),
            pl.BlockSpec((1, 1, KD), lambda i: (i, 0, 0)),
        ],
        out_shape=[
            jax.ShapeDtypeStruct((length, VD), F32),
            jax.ShapeDtypeStruct((length, KD), F32),
            jax.ShapeDtypeStruct((count, VD, KD), F32),
            jax.ShapeDtypeStruct((VD, KD), F32),
            jax.ShapeDtypeStruct((1, KD), F32),
            jax.ShapeDtypeStruct((count, 1, KD), F32),
        ],
        scratch_shapes=[pltpu.VMEM((VD, KD), F32), pltpu.VMEM((8, KD), F32)],
        compiler_params=pltpu.CompilerParams(
            dimension_semantics=("arbitrary",), vmem_limit_bytes=32 * 2**20
        ),
        cost_estimate=cost(Order.cost_f),
        name="mixer_forward",
    )(projected, projected, projected, decay)


def mixer_backward(projected, decay, grad, states, prefix, earlier, later):
    length = decay.shape[0]
    count = length // BLOCK_LEN
    row = lambda i: (count - 1 - i, 0)
    fixed = lambda i: (0, 0)
    return pl.pallas_call(
        backward_kernel,
        grid=(count,),
        in_specs=[
            pl.BlockSpec((BLOCK_LEN, KD), lambda i: (count - 1 - i, 0)),
            pl.BlockSpec((BLOCK_LEN, KD), lambda i: (count - 1 - i, 1)),
            pl.BlockSpec((BLOCK_LEN, VD), lambda i: (count - 1 - i, 1)),
            pl.BlockSpec((BLOCK_LEN, KD), row),
            pl.BlockSpec((BLOCK_LEN, VD), row),
            pl.BlockSpec((1, VD, KD), lambda i: (count - 1 - i, 0, 0)),
            pl.BlockSpec((1, 1, KD), lambda i: (count - 1 - i, 0, 0)),
            pl.BlockSpec((VD, KD), fixed),
            pl.BlockSpec((VD, KD), fixed),
        ],
        out_specs=[
            pl.BlockSpec((BLOCK_LEN, 2 * KD + VD), row),
            pl.BlockSpec((BLOCK_LEN, KD), row),
        ],
        out_shape=[
            jax.ShapeDtypeStruct((length, 2 * KD + VD), BF16),
            jax.ShapeDtypeStruct((length, KD), F32),
        ],
        scratch_shapes=[pltpu.VMEM((VD, KD), F32)],
        compiler_params=pltpu.CompilerParams(
            dimension_semantics=("arbitrary",), vmem_limit_bytes=32 * 2**20
        ),
        cost_estimate=cost(Order.cost_b),
        name="mixer_backward",
    )(projected, projected, projected, decay, grad, states, prefix, earlier, later)


def chip_bits():
    bits, bit = [], 2
    while bit < lax.axis_size("seq"):
        bits.append(bit)
        bit *= 2
    return bits


def tie(arrays, *first):
    return lax.optimization_barrier((arrays, first))[0]


def hop(x, step):
    bits = chip_bits()
    there = (bits[step], bits[-1 - step])
    count = lax.axis_size("seq")
    return lax.ppermute(x, "seq", [(i, i ^ there[i % 2]) for i in range(count)])


def place_in(core_order):
    count = len(chip_bits())
    return sum(((core_order >> k) & 1) << (count - 1 - k) for k in range(count))


def same_order(parts, core):
    return [
        x if place_in(i) == i else jnp.where(core == 0, x, parts[place_in(i)])
        for i, x in enumerate(parts)
    ]


class Spread:
    def __init__(self, rows):
        self.parts = [rows]
        self.steps = 0

    def load(self):
        return self.parts[0] if len(self.parts) == 1 else jnp.concatenate(self.parts, 0)

    def take(self, got):
        rows = self.parts[0].shape[0]
        count = len(self.parts)
        self.parts = self.parts + [got[i * rows : (i + 1) * rows] for i in range(count)]
        self.steps += 1


class Collect:
    def __init__(self, rows):
        self.rows = rows
        self.steps = 0

    def load(self):
        return self.rows[self.rows.shape[0] // 2 :]

    def take(self, got):
        kept = self.rows[: self.rows.shape[0] // 2].astype(F32)
        self.rows = (kept + got.astype(F32)).astype(BF16)
        self.steps += 1


class Plane:
    def __init__(self, plan, reverse=False):
        names = sorted({name for slot in plan for name, _ in slot}, key=str(plan).index)
        steps = len(chip_bits())
        self.plan = plan if steps == 2 else [[(n, i)] for n in names for i in range(steps)]
        self.phases = {}
        self.reverse = reverse
        self.done = []

    def slot(self, *first):
        now = self.plan[len(self.done)]
        loads = [self.phases[name].load() for name, _ in now]
        if len(self.done) >= 2 and Order.lag:
            first = first + (self.done[-2],)
        if first:
            loads = tie(loads, *first)
        landed = []
        for (name, i), x in zip(now, loads):
            got = hop(x, len(chip_bits()) - 1 - i if self.reverse else i)
            self.phases[name].take(got)
            landed.append(got)
        self.done.append(landed)

    def until(self, *names):
        while any(self.phases[name].steps < len(chip_bits()) for name in names):
            self.slot()


def order():
    chip, dp = lax.axis_index("seq") // 2, lax.axis_index("dp")
    near = [0]
    for bit in chip_bits():
        near = near + [place ^ (bit // 2) for place in near]
    chips = len(near)
    return [(dp ^ away) * chips + (chip ^ place) for away in range(2) for place in near]


def reorder_kernel(count, index_ref, *refs):
    half = len(refs) // 2
    for source, target in zip(refs[:half], refs[half:]):
        width = source.shape[1] // count
        for i in range(count):
            start = pl.multiple_of(index_ref[i] * width, width)
            target[:, i * width : (i + 1) * width] = source[:, pl.ds(start, width)]


def reorder(index, *arrays):
    count = index.shape[0]
    rows, columns = arrays[0].shape
    if (columns // count) % 128:
        moved = [
            jnp.take(x.reshape(rows, count, -1), index, axis=1).reshape(rows, columns)
            for x in arrays
        ]
        return moved
    step = rows // 3 if rows % 48 == 0 else rows
    spec = pl.BlockSpec((step, columns), lambda i, _: (i, 0))
    return pl.pallas_call(
        functools.partial(reorder_kernel, count),
        grid_spec=pltpu.PrefetchScalarGridSpec(
            num_scalar_prefetch=1,
            grid=(rows // step,),
            in_specs=[spec] * len(arrays),
            out_specs=[spec] * len(arrays),
        ),
        out_shape=[jax.ShapeDtypeStruct(x.shape, x.dtype) for x in arrays],
        compiler_params=pltpu.CompilerParams(
            dimension_semantics=("arbitrary",), vmem_limit_bytes=32 * 2**20
        ),
        name="reorder",
    )(index, *arrays)


def core_order(x, core):
    count = 2 * 2 ** len(chip_bits())
    parts = jnp.split(x, count, 1)
    half = count // 2
    return jnp.concatenate(same_order(parts[:half], core) + same_order(parts[half:], core), 1)


def halves(pairs):
    half = pairs[0][0].shape[1] // 2

    def part(i):
        grads = [inner(left[:, i * half : (i + 1) * half], right) for left, right in pairs]
        return jnp.concatenate([grad.astype(BF16) for grad in grads], 1)

    return Collect(part(1)), Collect(part(0))


def both(x, core):
    other = swap(x, "seq", CORE)
    return jnp.concatenate([jnp.where(core == 0, x, other), jnp.where(core == 0, other, x)], 0)


def core_sum(part, core):
    rows = part.shape[0] // 2
    mine = jnp.where(core == 0, part[:rows], part[rows:])
    theirs = jnp.where(core == 0, part[rows:], part[:rows])
    mine = mine + swap(theirs.astype(BF16), "seq", CORE).astype(F32)
    return mine.astype(BF16)


def add_up(part, core):
    mine = core_sum(part, core)
    return mine.astype(F32) + swap(mine, "head").astype(F32)


def incoming(edge, state, reverse=False):
    chips = lax.axis_size("seq") // 2
    rows = state.shape[0]
    high = edge.astype(BF16)
    low = (edge - high.astype(F32)).astype(BF16)
    edges = jnp.pad(jnp.concatenate([high, low], 0), ((0, 14), (0, 0)))
    packed = jnp.concatenate([state.astype(BF16), edges], 0)

    def move(by):
        by = -by if reverse else by
        pairs = []
        for i in range(chips):
            if 0 <= i + by < chips:
                for c in range(2):
                    pairs.append((2 * i + c, 2 * (i + by) + c))
        return lax.ppermute(packed, "seq", pairs).astype(F32)

    total, faded = jnp.zeros_like(state), None
    for by in range(1, chips):
        there = move(by)
        gone = there[rows : rows + 1] + there[rows + 1 : rows + 2]
        if by == 1:
            total, faded = there[:rows], gone
        else:
            total, faded = total + faded * there[:rows], faded * gone
    return total


def body(
    tokens,
    mix_gain,
    w_query,
    w_key,
    w_value,
    w_outgate,
    w_lowrank,
    w_rate,
    rate_bias,
    head_gain,
    w_output,
    mlp_gain,
    w_gate,
    w_up,
    w_down,
    cotangent,
):
    core = lax.axis_index("seq") % 2
    blocks = order()
    wide = tokens.shape[1] // (2 * len(blocks))
    place_of = jnp.stack(blocks).astype(jnp.int32)
    places = jnp.arange(len(blocks), dtype=jnp.int32)
    back_place = jnp.sum(
        jnp.where(place_of[None] == places[:, None], places[None], 0), axis=1, dtype=jnp.int32
    )

    def split(w):
        half = w.shape[1] // 2
        mine = jnp.where(core == 0, w[:, :half], w[:, half:])
        theirs = jnp.where(core == 0, w[:, half:], w[:, :half])
        return mine, theirs

    def own_columns(weights, shared=()):
        pairs = [split(w) for w in weights] + [(w, w) for w in shared]
        mine = jnp.concatenate([p[0] for p in pairs], 1)
        got = swap(jnp.concatenate([p[1] for p in pairs], 1), "seq", CORE)
        return jnp.concatenate(
            [jnp.where(core == 0, mine, got), jnp.where(core == 0, got, mine)], 0
        )

    bits = len(chip_bits())
    phases = {}
    seen = Seen()

    def after(x, key):
        first = [y for y in key(seen) if not (isinstance(y, tuple) and not y)]
        return tie(x, *first) if first else x

    def exchange(x, key):
        count = getattr(Order, key)
        size = x.shape[0] // count
        parts = [swap(x[i * size : (i + 1) * size], "head") for i in range(count)]
        for i, part in enumerate(parts):
            setattr(seen, key + str(i), part)
        return jnp.concatenate(parts, 0) if count > 1 else parts[0]

    def slot(hops, key):
        loads = after([phases[name].load() for name in hops], key)
        landed = []
        for name, x in zip(hops, loads):
            got = hop(x, phases[name].steps)
            phases[name].take(got)
            landed.append(got)
        return landed

    def rest_of(*names):
        for name in names:
            while phases[name].steps < bits:
                slot([name], Order.rest)

    def gathered(name, start, width):
        near = same_order([x[:, start : start + width] for x in phases[name].parts], core)
        far = same_order([x[:, start : start + width] for x in phases["far " + name].parts], core)
        return near + far

    low_pad = jnp.pad(w_lowrank, ((0, 0), (0, 128 - w_lowrank.shape[1])))
    hidden_width = w_gate.shape[1] // 2
    wide_mixer = 2 * KD + 2 * VD
    width = wide_mixer + 128
    fill = width - VD
    chip_mixer = own_columns([w_query, w_key, w_value, w_outgate], [low_pad])
    phases["mixer"] = Spread(chip_mixer)
    far_mixer = swap(chip_mixer, "dp")
    zero = slot(["mixer"], Order.rest)
    w_output, w_gate, w_up, w_down = tie((w_output, w_gate, w_up, w_down), chip_mixer)
    chip_gate = own_columns([w_gate])
    chip_two = jnp.concatenate([own_columns([w_output.T]), chip_gate[:, :fill]], 1)
    chip_three = jnp.concatenate([chip_gate[:, fill:], own_columns([w_up])], 1)
    chip_down = own_columns([w_down.T])
    phases["two"], phases["three"] = Spread(chip_two), Spread(chip_three)
    phases["down"] = Spread(chip_down)
    zero += slot(["two", "three", "down"], Order.rest)
    seen.zero, seen.far_mixer = zero, far_mixer
    tokens, cotangent = tie((tokens, cotangent), chip_down)
    phases["far mixer"] = Spread(far_mixer)
    far_two = swap(after(chip_two, Order.far_two), "dp")
    seen.one = slot(["far mixer", "mixer", "two"], Order.one)
    rest_of("mixer", "two")
    seen.far_two = far_two
    phases["far two"] = Spread(far_two)
    far_three = swap(after(chip_three, Order.far_three), "dp")
    seen.two = slot(["far mixer", "far two", "three"], Order.two)
    rest_of("far mixer", "three")
    if bits > 2:
        rest_of("far two")
    seen.far_three = far_three
    phases["far three"] = Spread(far_three)
    w_mixer = jnp.concatenate(gathered("mixer", 0, width), 0)

    cot, low_tokens = reorder(place_of, cotangent, tokens)
    gains = jnp.concatenate([mix_gain[None], mlp_gain[None]], 0)
    gains = reorder(place_of, jnp.pad(gains, ((0, 6), (0, 0))))[0]
    gain1, gain2 = gains[0], gains[1]
    cot_both = both(cot, core)
    inputs = low_tokens.astype(F32)
    length = 2 * tokens.shape[0]

    normed, norm_back = jax.vjp(rms_norm, inputs, gain1)
    normed_own = normed.astype(BF16)
    normed_low = both(normed_own, core)
    projected = matmul(after(normed_low, Order.projected), w_mixer)
    outgate = projected[:, 2 * KD + VD : wide_mixer]
    rank = w_lowrank.shape[1]
    rank_part = projected[:, wide_mixer : wide_mixer + rank].astype(BF16)
    rate = jnp.where(core == 0, w_rate[:, :KD], w_rate[:, KD:])
    bias = jnp.where(core == 0, rate_bias[:KD], rate_bias[KD:])
    logit = matmul(rank_part, rate) + bias
    decay = jax.nn.log_sigmoid(logit) / normalizer
    local_output, lifted, states, state_end, edge, fades = mixer_forward(projected, decay)
    seen.state = state_end
    far_down = swap(after(chip_down, Order.far_down), "dp")
    seen.three = slot(
        (["far two", "far three"] if bits == 2 else ["far three"]) + ["down"] * Order.early, Order.three
    )
    rest_of("far two")
    phases["far down"] = Spread(far_down)
    incoming_state = incoming(edge, state_end)
    seen.incoming = incoming_state
    mixed_output = local_output + dot(lifted, after(incoming_state, Order.mixed), (1, 1), PASSES)
    seen.far_down = far_down
    seen.four = slot(["far three"] + ["down"] * (1 - Order.early) + ["far down"], Order.four)
    rest_of("far three", "down")
    w_out = jnp.concatenate(gathered("two", 0, VD), 0)
    gated, gated_back = jax.vjp(head_norm, mixed_output, outgate, head_gain)
    gated_low = gated.astype(BF16)
    mixer_chip = core_sum(times_back(gated_low, w_out), core)
    seen.chip = mixer_chip
    mixer_head = exchange(mixer_chip, "pieces_a")
    seen.head = mixer_head
    seen.five = slot(["far down"], Order.five)
    rest_of("far down")
    middle = inputs + (mixer_chip.astype(F32) + mixer_head.astype(F32))
    rest = hidden_width - fill
    full_gate = jnp.concatenate(
        [
            jnp.concatenate(pair, 1)
            for pair in zip(gathered("two", VD, fill), gathered("three", 0, rest))
        ],
        0,
    )
    full_up = jnp.concatenate(gathered("three", rest, hidden_width), 0)
    w_dn = jnp.concatenate(gathered("down", 0, hidden_width), 0)
    normed2, norm2_back = jax.vjp(rms_norm, middle, gain2)
    normed2_low = both(normed2.astype(BF16), core)
    normed2_low = after(normed2_low, Order.gate)
    gate = matmul(normed2_low, full_gate)
    upward = matmul(normed2_low, full_up)
    hidden_low = swiglu(gate, upward).astype(BF16)
    cot_core = core_order(cot_both, core)
    normed_core = core_order(normed_low, core)
    normed2_core = core_order(normed2_low, core)
    back = Plane(
        [
            [("far down", 0)],
            [("down", 0)],
            [("far gate", 0), ("far down", 1)],
            [("gate", 0), ("down", 1)],
            [("far up", 0), ("far gate", 1)],
            [("up", 0), ("gate", 1)],
            [("far output", 0), ("far up", 1)],
            [("output", 0), ("up", 1)],
            [("far qkv", 0), ("far output", 1)],
            [("qkv", 0), ("output", 1)],
            [("far qkv", 1)],
            [("qkv", 1)],
        ],
        reverse=True,
    )
    sums = back.phases
    sums["far down"], sums["down"] = halves([(cot_core, hidden_low)])
    down_rows = sums["far down"].rows, sums["down"].rows
    seen.D = down_rows

    def go(key):
        first = getattr(Order, key)(seen)
        back.slot(*[y for y in first if not (isinstance(y, tuple) and not y)])
        setattr(seen, key, back.done[-1])

    def far_sum(name, key):
        return swap(after(sums["far " + name].rows.astype(BF16), key), "dp")

    go("b0")
    go("b1")
    grad_result, gate, upward, full_gate, full_up = after(
        tie((cot_both, gate, upward, full_gate, full_up), w_dn, down_rows), Order.hidden
    )
    grad_hidden = matmul(grad_result, w_dn)
    sigma = jax.nn.sigmoid(gate)
    gate_low = (grad_hidden * upward * sigma * (1.0 + gate * (1.0 - sigma))).astype(BF16)
    upward_low = (grad_hidden * gate * sigma).astype(BF16)
    sums["far gate"], sums["gate"] = halves([(normed2_core, after(gate_low, Order.G_dots))])
    seen.G = sums["far gate"].rows, sums["gate"].rows
    part = times_back(after(gate_low, Order.part_gate), full_gate) + times_back(
        after(upward_low, Order.part_up), full_up
    )
    chip_sum = core_sum(part, core)
    seen.chip2 = chip_sum
    head_part = exchange(chip_sum, "pieces_b")
    seen.head2 = head_part
    sums["far up"], sums["up"] = halves([(normed2_core, after(upward_low, Order.U_dots))])
    seen.U = sums["far up"].rows, sums["up"].rows
    go("b2")
    go("b3")
    feed_chip = core_sum(times_back(after(hidden_low, Order.feed), w_dn), core)
    seen.feed = feed_chip
    go("b4")
    feed_head = swap(after(feed_chip, Order.feed_head), "head")
    grad_normed2 = chip_sum.astype(F32) + after(head_part, Order.norm2).astype(F32)
    middle_grad, grad_mlp_gain = norm2_back(grad_normed2)
    grad_middle = cot.astype(F32) + middle_grad
    middle_low = both(grad_middle.astype(BF16), core)
    seen.middle = middle_low
    grad_gated = matmul(after(middle_low, Order.gated), w_out)
    mixed_gradient, outgate_grad, head_gain_part = gated_back(grad_gated)
    outgate_low = outgate_grad.astype(BF16)
    middle_core = core_order(middle_low, core)
    contribution = dot(mixed_gradient, lifted, (0, 0), PASSES)
    seen.contribution = contribution
    go("b5")
    outgoing = incoming(edge, contribution, reverse=True)
    seen.outgoing = outgoing
    far_sums = {}
    if bits == 2:
        far_sums["down"], far_sums["gate"] = far_sum("down", Order.dp_D), far_sum("gate", Order.dp_G)
        seen.D_sum, seen.G_sum = far_sums["down"], far_sums["gate"]
    outgate_late = after(outgate_low, Order.O_dots)
    sums["far output"], sums["output"] = halves(
        [(middle_core, gated_low), (normed_core, outgate_late)]
    )
    seen.O = sums["far output"].rows, sums["output"].rows
    if bits == 2:
        go("b6")
    outgoing = after(outgoing, Order.kernel)
    qkv_low, decay_grad = mixer_backward(
        projected, decay, mixed_gradient, states, fades, incoming_state, outgoing
    )
    logit_low = (decay_grad * jax.nn.sigmoid(-logit) / normalizer).astype(BF16)
    grad_rate = inner(rank_part, logit_low)
    grad_rate_bias = jnp.sum(logit_low.astype(F32), axis=0)
    rank_low = times_back(logit_low, rate).astype(BF16)
    rank_low = jnp.pad(rank_low, ((0, 0), (0, 128 - rank)))
    mixer_low = jnp.concatenate([qkv_low, outgate_low, rank_low], 1)
    seen.qkv = qkv_low
    normed_chip = core_sum(times_back(after(mixer_low, Order.normed), w_mixer), core)
    seen.chip3 = normed_chip
    normed_head = exchange(normed_chip, "pieces_c")
    seen.head3 = normed_head
    qkv_rank = after(jnp.concatenate([qkv_low, rank_low], 1), Order.Q_dots)
    feed_head = after(feed_head, Order.result)
    result = (middle + (feed_chip.astype(F32) + feed_head.astype(F32))).astype(BF16)
    result = reorder(back_place, result)[0]
    seen.result_ = result
    sums["far qkv"], sums["qkv"] = halves([(normed_core, qkv_rank)])
    seen.Q = sums["far qkv"].rows, sums["qkv"].rows
    if bits == 2:
        go("b7")
    go("b8")
    go("b9")
    go("b10")
    if bits == 2:
        far_sums["qkv"] = far_sum("qkv", Order.dp_Q)
        seen.Q_sum = far_sums["qkv"]
    go("b11")
    back.until(*sums)
    if bits == 2:
        far_sums["up"], far_sums["output"] = far_sum("up", Order.dp_U), far_sum("output", Order.dp_O)
        seen.U_sum, seen.O_sum = far_sums["up"], far_sums["output"]
    normed_head = after(normed_head, Order.tail)
    grad_normed = normed_chip.astype(F32) + normed_head.astype(F32)
    inputs_grad, grad_mix_gain = norm_back(grad_normed)
    grad_tokens = reorder(back_place, grad_middle + inputs_grad)[0]

    finished = []
    for name in ("down", "gate", "up", "output", "qkv"):
        got = far_sums[name] if name in far_sums else far_sum(name, Order.rest)
        got = after(got, getattr(Order, "end_" + name))
        finished.append(sums[name].rows.astype(F32) + got.astype(F32))
    grad_down, grad_gate, grad_up, grad_output, grad_qkv = finished

    def own_rows(chip_rows):
        mine = jnp.where(core == 0, chip_rows[:wide], chip_rows[wide:])
        theirs = jnp.where(core == 0, chip_rows[wide:], chip_rows[:wide])
        got = swap(theirs.astype(BF16), "seq", CORE).astype(F32)
        return jnp.where(core == 0, mine, got), jnp.where(core == 0, got, mine)

    def columns(pair, start, width):
        return jnp.concatenate([part[:, start : start + width] for part in pair], 1)

    qkv_pair = own_rows(grad_qkv[:, : 2 * KD + VD])
    sum_query = columns(qkv_pair, 0, KD)
    sum_key = columns(qkv_pair, KD, KD)
    sum_value = columns(qkv_pair, 2 * KD, VD)
    low_rows = grad_qkv[:, 2 * KD + VD : 2 * KD + VD + rank]
    low_mine = jnp.where(core == 0, low_rows[:wide], low_rows[wide:])
    low_theirs = jnp.where(core == 0, low_rows[wide:], low_rows[:wide])
    low_mine = low_mine + swap(low_theirs, "seq", CORE)
    sum_lowrank = low_mine + swap(low_mine, "head")
    output_pair = own_rows(grad_output)
    sum_output = columns(output_pair, 0, VD).T
    sum_outgate = columns(output_pair, VD, VD)
    sum_gate = jnp.concatenate(own_rows(grad_gate), 1)
    sum_up = jnp.concatenate(own_rows(grad_up), 1)
    sum_down = jnp.concatenate(own_rows(grad_down), 1).T

    zero = jnp.zeros_like(grad_rate)
    wide_rate = jnp.where(
        core == 0,
        jnp.concatenate([grad_rate, zero], 1),
        jnp.concatenate([zero, grad_rate], 1),
    )
    wide_bias = jnp.where(
        core == 0,
        jnp.concatenate([grad_rate_bias, zero[0]]),
        jnp.concatenate([zero[0], grad_rate_bias]),
    )
    head_gain_part = head_gain_part + swap(head_gain_part[None], "head")[0]
    gain_rows = jnp.stack([grad_mix_gain, grad_mlp_gain])
    gain_rows = reorder(back_place, jnp.pad(gain_rows, ((0, 6), (0, 0))))[0][:2]
    model = gain_rows.shape[1]
    others = jnp.concatenate([wide_bias, head_gain_part])
    others = jnp.pad(others, (0, 2 * model - others.shape[0])).reshape(2, model)
    others = jnp.concatenate([others, wide_rate.reshape(-1, model)], 0)
    small = jnp.concatenate([gain_rows, others], 0)
    for axis, axis_bits in (("seq", [CORE] + chip_bits()), ("dp", [1])):
        for bit in axis_bits:
            small = small + swap(small, axis, bit)
    sum_mix_gain, sum_mlp_gain = small[0], small[1]
    sum_rate_bias = small[2, : wide_bias.size]
    sum_head_gain = small[2, wide_bias.size : wide_bias.size + VD]
    sum_rate = small[4:].reshape(wide_rate.shape)
    return (
        result,
        grad_tokens,
        sum_mix_gain,
        sum_query,
        sum_key,
        sum_value,
        sum_outgate,
        sum_lowrank,
        sum_rate,
        sum_rate_bias,
        sum_head_gain,
        sum_output,
        sum_mlp_gain,
        sum_gate,
        sum_up,
        sum_down,
    )


def solution(mesh):
    rows = P(("dp", "seq"), None)
    in_columns = P(("dp", "seq"), "head")
    in_rows = P("head", ("dp", "seq"))
    in_specs = (
        rows,
        P(),
        in_columns,
        in_columns,
        in_columns,
        in_columns,
        rows,
        P(None, "head"),
        P("head"),
        P(),
        in_rows,
        P(),
        in_columns,
        in_columns,
        in_rows,
        rows,
    )
    out_specs = (
        rows,
        rows,
        P(),
        in_columns,
        in_columns,
        in_columns,
        in_columns,
        rows,
        P(None, "head"),
        P("head"),
        P(),
        in_rows,
        P(),
        in_columns,
        in_columns,
        in_rows,
    )
    return jax.shard_map(body, mesh=mesh, in_specs=in_specs, out_specs=out_specs, check_vma=False)
```

```python
import functools

import jax
import jax.numpy as jnp
from jax import lax
from jax.experimental import pallas as pl
from jax.experimental.pallas import tpu as pltpu
from jax.sharding import PartitionSpec as P

KD = 256
VD = 512
BLOCK_LEN = 64

epsilon = 1e-06
normalizer = 16.0
MATMUL_PRECISION = lax.Precision.HIGHEST
BF16 = jnp.bfloat16
F32 = jnp.float32
CORE = 1


class Order:
    rest = lambda at: ()
    lag = 0
    early = 0
    pieces_a = 1
    pieces_b = 1
    pieces_c = 1
    far_two = lambda at: (at.far_mixer,)
    one = lambda at: (at.zero, at.far_mixer,)
    far_three = lambda at: (at.one, at.far_two,)
    two = lambda at: (at.one, at.far_two,)
    projected = lambda at: ()
    far_down = lambda at: (at.two, at.far_three, at.state,)
    three = lambda at: (at.two, at.far_three, at.state,)
    mixed = lambda at: ()
    four = lambda at: (at.three, at.far_down, at.incoming,)
    five = lambda at: (at.far_down,)
    gate = lambda at: (at.four,)
    b0 = lambda at: (at.five,)
    b1 = lambda at: ()
    hidden = lambda at: ()
    G_dots = lambda at: ()
    part_gate = lambda at: (at.G, at.b0,)
    part_up = lambda at: (at.G,)
    U_dots = lambda at: (at.chip2,)
    b2 = lambda at: ()
    b3 = lambda at: (at.chip2,)
    feed = lambda at: (at.U, at.b2,)
    b4 = lambda at: (at.head2,)
    feed_head = lambda at: (at.head2,)
    norm2 = lambda at: ()
    gated = lambda at: ()
    b5 = lambda at: (at.feed,)
    dp_D = lambda at: (at.head2,)
    dp_G = lambda at: ()
    O_dots = lambda at: (at.contribution, at.D_sum,)
    b6 = lambda at: (at.outgoing,)
    kernel = lambda at: (at.O, at.b5, at.G_sum,)
    normed = lambda at: (at.b5,)
    Q_dots = lambda at: (at.chip3,)
    result = lambda at: (at.qkv,)
    b7 = lambda at: (at.chip3,)
    b8 = lambda at: ()
    b9 = lambda at: ()
    b10 = lambda at: (at.head3,)
    b11 = lambda at: (at.head3,)
    dp_Q = lambda at: (at.head3,)
    dp_U = lambda at: ()
    dp_O = lambda at: ()
    tail = lambda at: (at.b11, at.b9,)
    end_down = lambda at: (at.chip3,)
    end_gate = lambda at: (at.qkv,)
    end_up = lambda at: (at.b9,)
    end_output = lambda at: ()
    end_qkv = lambda at: ()
    cost_f = 0
    cost_b = 0
    core = 1


class Seen:
    def __getattr__(self, name):
        return ()


def swap(x, axis, bit=1):
    count = lax.axis_size(axis)
    return lax.ppermute(x, axis, [(i, i ^ bit) for i in range(count)])


def matmul(left, right):
    return jnp.dot(left, right, preferred_element_type=F32)


def inner(left, right):
    return lax.dot_general(left, right, (((0,), (0,)), ((), ())), preferred_element_type=F32)


def times_back(grad, weight):
    return lax.dot_general(grad, weight, (((1,), (1,)), ((), ())), preferred_element_type=F32)


def rms_norm(x, gain):
    return x * lax.rsqrt(jnp.mean(x * x, axis=-1, keepdims=True) + epsilon) * gain


def head_norm(mixed_output, outgate, gain):
    return rms_norm(mixed_output, gain) * jax.nn.silu(outgate)


def swiglu(gate, upward):
    return jax.nn.silu(gate) * upward


def dot(a, b, contract, passes=1):
    dims = ((contract[0],), (contract[1],)), ((), ())

    def once(x, y):
        return lax.dot_general(x, y, dims, preferred_element_type=F32)

    high_a, high_b = a.astype(BF16), b.astype(BF16)
    total = once(high_a, high_b)
    if passes > 1:
        low_a = (a - high_a.astype(F32)).astype(BF16)
        low_b = (b - high_b.astype(F32)).astype(BF16)
        total = total + (once(high_a, low_b) + once(low_a, high_b))
    return total


def triangle(size):
    rows = lax.broadcasted_iota(jnp.int32, (size, size), 0)
    columns = lax.broadcasted_iota(jnp.int32, (size, size), 1)
    return rows >= columns


def block_terms(query, key, decay):
    size = decay.shape[0]
    ones = jnp.where(triangle(size), 1.0, 0.0)
    running = lax.dot_general(
        ones, decay, (((1,), (0,)), ((), ())), precision=MATMUL_PRECISION, preferred_element_type=F32
    )
    final = running[size - 1 : size]
    rise, fall, rest = jnp.exp(running), jnp.exp(-running), jnp.exp(final - running)
    return query * (KD**-0.5) * rise, key * fall, key * rest, rise, fall, rest, final


PASSES = 1


def forward_kernel(q_ref, k_ref, v_ref, d_ref, out_ref, lifted_ref, states_ref, end_ref, edge_ref, prefix_ref, state, before):
    @pl.when(pl.program_id(0) == 0)
    def _():
        state[...] = jnp.zeros_like(state)
        before[...] = jnp.zeros_like(before)

    lifted, lowered, carried, _, _, _, final = block_terms(q_ref[...], k_ref[...], d_ref[...])
    value = v_ref[...]
    scores = dot(lifted, lowered, (1, 1), PASSES)
    scores = jnp.where(triangle(scores.shape[0]), scores, 0.0)
    held = state[...]
    out_ref[...] = dot(scores, value, (1, 0), PASSES) + dot(lifted, held, (1, 1), PASSES)
    reach = jnp.exp(before[0:1])
    lifted_ref[...] = lifted * reach
    prefix_ref[...] = reach[None]
    states_ref[...] = held[None]
    new = held * jnp.exp(final) + dot(value, carried, (0, 0), PASSES)
    state[...] = new
    before[0:1] = before[0:1] + final
    end_ref[...] = new
    edge_ref[...] = jnp.exp(before[0:1])


def backward_kernel(q_ref, k_ref, v_ref, d_ref, grad_ref, states_ref, prefix_ref, in_ref, out_ref, mixer_ref, decay_ref, state):
    @pl.when(pl.program_id(0) == 0)
    def _():
        state[...] = out_ref[...]

    lifted, lowered, carried, rise, fall, rest, final = block_terms(q_ref[...], k_ref[...], d_ref[...])
    value, grad = v_ref[...], grad_ref[...]
    later = state[...]
    held = states_ref[0] + in_ref[...] * prefix_ref[0]
    lower = triangle(value.shape[0])
    scores = jnp.where(lower, dot(lifted, lowered, (1, 1), PASSES), 0.0)
    grad_scores = jnp.where(lower, dot(grad, value, (1, 1), PASSES), 0.0)
    grad_value = dot(scores, grad, (0, 0), PASSES) + dot(carried, later, (1, 1), PASSES)
    grad_lifted = dot(grad, held, (1, 0), PASSES) + dot(grad_scores, lowered, (1, 0), PASSES)
    grad_lowered = dot(grad_scores, lifted, (0, 0), PASSES)
    grad_carried = dot(value, later, (1, 0), PASSES)
    mixer_ref[:, :KD] = (grad_lifted * rise * (KD**-0.5)).astype(BF16)
    mixer_ref[:, KD : 2 * KD] = (grad_lowered * fall + grad_carried * rest).astype(BF16)
    mixer_ref[:, 2 * KD :] = grad_value.astype(BF16)
    through = carried * grad_carried
    change = lifted * grad_lifted - lowered * grad_lowered - through
    fade = jnp.exp(final)
    last = jnp.sum(through, axis=0, keepdims=True) + fade * jnp.sum(held * later, axis=0, keepdims=True)
    ones = jnp.where(lower, 1.0, 0.0)
    decay_ref[...] = last + lax.dot_general(
        ones, change, (((0,), (0,)), ((), ())), precision=MATMUL_PRECISION, preferred_element_type=F32
    )
    state[...] = later * fade + dot(grad, lifted, (0, 0), PASSES)


def cost(key):
    flops = (None, 10**6, 2 * 10**10)[key]
    if flops is None:
        return None
    return pl.CostEstimate(flops=flops, bytes_accessed=10**5, transcendentals=0)


def mixer_forward(projected, decay):
    length = decay.shape[0]
    count = length // BLOCK_LEN
    row = lambda i: (i, 0)
    fixed = lambda i: (0, 0)
    return pl.pallas_call(
        forward_kernel,
        grid=(count,),
        in_specs=[
            pl.BlockSpec((BLOCK_LEN, KD), lambda i: (i, 0)),
            pl.BlockSpec((BLOCK_LEN, KD), lambda i: (i, 1)),
            pl.BlockSpec((BLOCK_LEN, VD), lambda i: (i, 1)),
            pl.BlockSpec((BLOCK_LEN, KD), row),
        ],
        out_specs=[
            pl.BlockSpec((BLOCK_LEN, VD), row),
            pl.BlockSpec((BLOCK_LEN, KD), row),
            pl.BlockSpec((1, VD, KD), lambda i: (i, 0, 0)),
            pl.BlockSpec((VD, KD), fixed),
            pl.BlockSpec((1, KD), fixed),
            pl.BlockSpec((1, 1, KD), lambda i: (i, 0, 0)),
        ],
        out_shape=[
            jax.ShapeDtypeStruct((length, VD), F32),
            jax.ShapeDtypeStruct((length, KD), F32),
            jax.ShapeDtypeStruct((count, VD, KD), F32),
            jax.ShapeDtypeStruct((VD, KD), F32),
            jax.ShapeDtypeStruct((1, KD), F32),
            jax.ShapeDtypeStruct((count, 1, KD), F32),
        ],
        scratch_shapes=[pltpu.VMEM((VD, KD), F32), pltpu.VMEM((8, KD), F32)],
        compiler_params=pltpu.CompilerParams(
            dimension_semantics=("arbitrary",), vmem_limit_bytes=32 * 2**20
        ),
        cost_estimate=cost(Order.cost_f),
        name="mixer_forward",
    )(projected, projected, projected, decay)


def mixer_backward(projected, decay, grad, states, prefix, earlier, later):
    length = decay.shape[0]
    count = length // BLOCK_LEN
    row = lambda i: (count - 1 - i, 0)
    fixed = lambda i: (0, 0)
    return pl.pallas_call(
        backward_kernel,
        grid=(count,),
        in_specs=[
            pl.BlockSpec((BLOCK_LEN, KD), lambda i: (count - 1 - i, 0)),
            pl.BlockSpec((BLOCK_LEN, KD), lambda i: (count - 1 - i, 1)),
            pl.BlockSpec((BLOCK_LEN, VD), lambda i: (count - 1 - i, 1)),
            pl.BlockSpec((BLOCK_LEN, KD), row),
            pl.BlockSpec((BLOCK_LEN, VD), row),
            pl.BlockSpec((1, VD, KD), lambda i: (count - 1 - i, 0, 0)),
            pl.BlockSpec((1, 1, KD), lambda i: (count - 1 - i, 0, 0)),
            pl.BlockSpec((VD, KD), fixed),
            pl.BlockSpec((VD, KD), fixed),
        ],
        out_specs=[
            pl.BlockSpec((BLOCK_LEN, 2 * KD + VD), row),
            pl.BlockSpec((BLOCK_LEN, KD), row),
        ],
        out_shape=[
            jax.ShapeDtypeStruct((length, 2 * KD + VD), BF16),
            jax.ShapeDtypeStruct((length, KD), F32),
        ],
        scratch_shapes=[pltpu.VMEM((VD, KD), F32)],
        compiler_params=pltpu.CompilerParams(
            dimension_semantics=("arbitrary",), vmem_limit_bytes=32 * 2**20
        ),
        cost_estimate=cost(Order.cost_b),
        name="mixer_backward",
    )(projected, projected, projected, decay, grad, states, prefix, earlier, later)


def chip_bits():
    bits, bit = [], 2
    while bit < lax.axis_size("seq"):
        bits.append(bit)
        bit *= 2
    return bits


def tie(arrays, *first):
    return lax.optimization_barrier((arrays, first))[0]


def hop(x, step):
    bits = chip_bits()
    there = (bits[step], bits[-1 - step])
    count = lax.axis_size("seq")
    return lax.ppermute(x, "seq", [(i, i ^ there[i % 2]) for i in range(count)])


def place_in(core_order):
    count = len(chip_bits())
    return sum(((core_order >> k) & 1) << (count - 1 - k) for k in range(count))


def same_order(parts, core):
    return [
        x if place_in(i) == i else jnp.where(core == 0, x, parts[place_in(i)])
        for i, x in enumerate(parts)
    ]


class Spread:
    def __init__(self, rows):
        self.parts = [rows]
        self.steps = 0

    def load(self):
        return self.parts[0] if len(self.parts) == 1 else jnp.concatenate(self.parts, 0)

    def take(self, got):
        rows = self.parts[0].shape[0]
        count = len(self.parts)
        self.parts = self.parts + [got[i * rows : (i + 1) * rows] for i in range(count)]
        self.steps += 1


class Collect:
    def __init__(self, rows):
        self.rows = rows
        self.steps = 0

    def load(self):
        return self.rows[self.rows.shape[0] // 2 :]

    def take(self, got):
        kept = self.rows[: self.rows.shape[0] // 2].astype(F32)
        self.rows = (kept + got.astype(F32)).astype(BF16)
        self.steps += 1


class Plane:
    def __init__(self, plan, reverse=False):
        names = sorted({name for slot in plan for name, _ in slot}, key=str(plan).index)
        steps = len(chip_bits())
        self.plan = plan if steps == 2 else [[(n, i)] for n in names for i in range(steps)]
        self.phases = {}
        self.reverse = reverse
        self.done = []

    def slot(self, *first):
        now = self.plan[len(self.done)]
        loads = [self.phases[name].load() for name, _ in now]
        if len(self.done) >= 2 and Order.lag:
            first = first + (self.done[-2],)
        if first:
            loads = tie(loads, *first)
        landed = []
        for (name, i), x in zip(now, loads):
            got = hop(x, len(chip_bits()) - 1 - i if self.reverse else i)
            self.phases[name].take(got)
            landed.append(got)
        self.done.append(landed)

    def until(self, *names):
        while any(self.phases[name].steps < len(chip_bits()) for name in names):
            self.slot()


def order():
    chip, dp = lax.axis_index("seq") // 2, lax.axis_index("dp")
    near = [0]
    for bit in chip_bits():
        near = near + [place ^ (bit // 2) for place in near]
    chips = len(near)
    return [(dp ^ away) * chips + (chip ^ place) for away in range(2) for place in near]


def reorder_kernel(count, index_ref, *refs):
    half = len(refs) // 2
    for source, target in zip(refs[:half], refs[half:]):
        width = source.shape[1] // count
        for i in range(count):
            start = pl.multiple_of(index_ref[i] * width, width)
            target[:, i * width : (i + 1) * width] = source[:, pl.ds(start, width)]


def reorder(index, *arrays):
    count = index.shape[0]
    rows, columns = arrays[0].shape
    if (columns // count) % 128:
        moved = [
            jnp.take(x.reshape(rows, count, -1), index, axis=1).reshape(rows, columns)
            for x in arrays
        ]
        return moved
    step = rows // 3 if rows % 48 == 0 else rows
    spec = pl.BlockSpec((step, columns), lambda i, _: (i, 0))
    return pl.pallas_call(
        functools.partial(reorder_kernel, count),
        grid_spec=pltpu.PrefetchScalarGridSpec(
            num_scalar_prefetch=1,
            grid=(rows // step,),
            in_specs=[spec] * len(arrays),
            out_specs=[spec] * len(arrays),
        ),
        out_shape=[jax.ShapeDtypeStruct(x.shape, x.dtype) for x in arrays],
        compiler_params=pltpu.CompilerParams(
            dimension_semantics=("arbitrary",), vmem_limit_bytes=32 * 2**20
        ),
        name="reorder",
    )(index, *arrays)


def core_order(x, core):
    count = 2 * 2 ** len(chip_bits())
    parts = jnp.split(x, count, 1)
    half = count // 2
    return jnp.concatenate(same_order(parts[:half], core) + same_order(parts[half:], core), 1)


def halves(pairs):
    half = pairs[0][0].shape[1] // 2

    def part(i):
        grads = [inner(left[:, i * half : (i + 1) * half], right) for left, right in pairs]
        return jnp.concatenate([grad.astype(BF16) for grad in grads], 1)

    return Collect(part(1)), Collect(part(0))


def both(x, core):
    other = swap(x, "seq", CORE)
    return jnp.concatenate([jnp.where(core == 0, x, other), jnp.where(core == 0, other, x)], 0)


def core_sum(part, core):
    rows = part.shape[0] // 2
    mine = jnp.where(core == 0, part[:rows], part[rows:])
    theirs = jnp.where(core == 0, part[rows:], part[:rows])
    mine = mine + swap(theirs.astype(BF16), "seq", CORE).astype(F32)
    return mine.astype(BF16)


def add_up(part, core):
    mine = core_sum(part, core)
    return mine.astype(F32) + swap(mine, "head").astype(F32)


def incoming(edge, state, reverse=False):
    chips = lax.axis_size("seq") // 2
    rows = state.shape[0]
    high = edge.astype(BF16)
    low = (edge - high.astype(F32)).astype(BF16)
    edges = jnp.pad(jnp.concatenate([high, low], 0), ((0, 14), (0, 0)))
    packed = jnp.concatenate([state.astype(BF16), edges], 0)

    def move(by):
        by = -by if reverse else by
        pairs = []
        for i in range(chips):
            if 0 <= i + by < chips:
                for c in range(2):
                    pairs.append((2 * i + c, 2 * (i + by) + c))
        return lax.ppermute(packed, "seq", pairs).astype(F32)

    total, faded = jnp.zeros_like(state), None
    for by in range(1, chips):
        there = move(by)
        gone = there[rows : rows + 1] + there[rows + 1 : rows + 2]
        if by == 1:
            total, faded = there[:rows], gone
        else:
            total, faded = total + faded * there[:rows], faded * gone
    return total


def body(
    tokens,
    mix_gain,
    w_query,
    w_key,
    w_value,
    w_outgate,
    w_lowrank,
    w_rate,
    rate_bias,
    head_gain,
    w_output,
    mlp_gain,
    w_gate,
    w_up,
    w_down,
    cotangent,
):
    core = lax.axis_index("seq") % 2
    blocks = order()
    wide = tokens.shape[1] // (2 * len(blocks))
    place_of = jnp.stack(blocks).astype(jnp.int32)
    places = jnp.arange(len(blocks), dtype=jnp.int32)
    back_place = jnp.sum(
        jnp.where(place_of[None] == places[:, None], places[None], 0), axis=1, dtype=jnp.int32
    )

    def split(w):
        half = w.shape[1] // 2
        mine = jnp.where(core == 0, w[:, :half], w[:, half:])
        theirs = jnp.where(core == 0, w[:, half:], w[:, :half])
        return mine, theirs

    def own_columns(weights, shared=()):
        pairs = [split(w) for w in weights] + [(w, w) for w in shared]
        mine = jnp.concatenate([p[0] for p in pairs], 1)
        got = swap(jnp.concatenate([p[1] for p in pairs], 1), "seq", CORE)
        return jnp.concatenate(
            [jnp.where(core == 0, mine, got), jnp.where(core == 0, got, mine)], 0
        )

    bits = len(chip_bits())
    phases = {}
    seen = Seen()

    def after(x, key):
        first = [y for y in key(seen) if not (isinstance(y, tuple) and not y)]
        return tie(x, *first) if first else x

    def exchange(x, key):
        count = getattr(Order, key)
        size = x.shape[0] // count
        parts = [swap(x[i * size : (i + 1) * size], "head") for i in range(count)]
        for i, part in enumerate(parts):
            setattr(seen, key + str(i), part)
        return jnp.concatenate(parts, 0) if count > 1 else parts[0]

    def slot(hops, key):
        loads = after([phases[name].load() for name in hops], key)
        landed = []
        for name, x in zip(hops, loads):
            got = hop(x, phases[name].steps)
            phases[name].take(got)
            landed.append(got)
        return landed

    def rest_of(*names):
        for name in names:
            while phases[name].steps < bits:
                slot([name], Order.rest)

    def gathered(name, start, width):
        near = same_order([x[:, start : start + width] for x in phases[name].parts], core)
        far = same_order([x[:, start : start + width] for x in phases["far " + name].parts], core)
        return near + far

    low_pad = jnp.pad(w_lowrank, ((0, 0), (0, 128 - w_lowrank.shape[1])))
    hidden_width = w_gate.shape[1] // 2
    wide_mixer = 2 * KD + 2 * VD
    width = wide_mixer + 128
    fill = width - VD
    chip_mixer = own_columns([w_query, w_key, w_value, w_outgate], [low_pad])
    phases["mixer"] = Spread(chip_mixer)
    far_mixer = swap(chip_mixer, "dp")
    zero = slot(["mixer"], Order.rest)
    w_output, w_gate, w_up, w_down = tie((w_output, w_gate, w_up, w_down), chip_mixer)
    chip_gate = own_columns([w_gate])
    chip_two = jnp.concatenate([own_columns([w_output.T]), chip_gate[:, :fill]], 1)
    chip_three = jnp.concatenate([chip_gate[:, fill:], own_columns([w_up])], 1)
    chip_down = own_columns([w_down.T])
    phases["two"], phases["three"] = Spread(chip_two), Spread(chip_three)
    phases["down"] = Spread(chip_down)
    zero += slot(["two", "three", "down"], Order.rest)
    seen.zero, seen.far_mixer = zero, far_mixer
    tokens, cotangent = tie((tokens, cotangent), chip_down)
    phases["far mixer"] = Spread(far_mixer)
    far_two = swap(after(chip_two, Order.far_two), "dp")
    seen.one = slot(["far mixer", "mixer", "two"], Order.one)
    rest_of("mixer", "two")
    seen.far_two = far_two
    phases["far two"] = Spread(far_two)
    far_three = swap(after(chip_three, Order.far_three), "dp")
    seen.two = slot(["far mixer", "far two", "three"], Order.two)
    rest_of("far mixer", "three")
    if bits > 2:
        rest_of("far two")
    seen.far_three = far_three
    phases["far three"] = Spread(far_three)
    w_mixer = jnp.concatenate(gathered("mixer", 0, width), 0)

    cot, low_tokens = reorder(place_of, cotangent, tokens)
    gains = jnp.concatenate([mix_gain[None], mlp_gain[None]], 0)
    gains = reorder(place_of, jnp.pad(gains, ((0, 6), (0, 0))))[0]
    gain1, gain2 = gains[0], gains[1]
    cot_both = both(cot, core)
    inputs = low_tokens.astype(F32)
    length = 2 * tokens.shape[0]

    normed, norm_back = jax.vjp(rms_norm, inputs, gain1)
    normed_own = normed.astype(BF16)
    normed_low = both(normed_own, core)
    projected = matmul(after(normed_low, Order.projected), w_mixer)
    outgate = projected[:, 2 * KD + VD : wide_mixer]
    rank = w_lowrank.shape[1]
    rank_part = projected[:, wide_mixer : wide_mixer + rank].astype(BF16)
    rate = jnp.where(core == 0, w_rate[:, :KD], w_rate[:, KD:])
    bias = jnp.where(core == 0, rate_bias[:KD], rate_bias[KD:])
    logit = matmul(rank_part, rate) + bias
    decay = jax.nn.log_sigmoid(logit) / normalizer
    local_output, lifted, states, state_end, edge, fades = mixer_forward(projected, decay)
    seen.state = state_end
    far_down = swap(after(chip_down, Order.far_down), "dp")
    seen.three = slot(
        (["far two", "far three"] if bits == 2 else ["far three"]) + ["down"] * Order.early, Order.three
    )
    rest_of("far two")
    phases["far down"] = Spread(far_down)
    incoming_state = incoming(edge, state_end)
    seen.incoming = incoming_state
    mixed_output = local_output + dot(lifted, after(incoming_state, Order.mixed), (1, 1), PASSES)
    seen.far_down = far_down
    seen.four = slot(["far three"] + ["down"] * (1 - Order.early) + ["far down"], Order.four)
    rest_of("far three", "down")
    w_out = jnp.concatenate(gathered("two", 0, VD), 0)
    gated, gated_back = jax.vjp(head_norm, mixed_output, outgate, head_gain)
    gated_low = gated.astype(BF16)
    mixer_chip = core_sum(times_back(gated_low, w_out), core)
    seen.chip = mixer_chip
    mixer_head = exchange(mixer_chip, "pieces_a")
    seen.head = mixer_head
    seen.five = slot(["far down"], Order.five)
    rest_of("far down")
    middle = inputs + (mixer_chip.astype(F32) + mixer_head.astype(F32))
    rest = hidden_width - fill
    full_gate = jnp.concatenate(
        [
            jnp.concatenate(pair, 1)
            for pair in zip(gathered("two", VD, fill), gathered("three", 0, rest))
        ],
        0,
    )
    full_up = jnp.concatenate(gathered("three", rest, hidden_width), 0)
    w_dn = jnp.concatenate(gathered("down", 0, hidden_width), 0)
    normed2, norm2_back = jax.vjp(rms_norm, middle, gain2)
    normed2_low = both(normed2.astype(BF16), core)
    normed2_low = after(normed2_low, Order.gate)
    gate = matmul(normed2_low, full_gate)
    upward = matmul(normed2_low, full_up)
    hidden_low = swiglu(gate, upward).astype(BF16)
    cot_core = core_order(cot_both, core)
    normed_core = core_order(normed_low, core)
    normed2_core = core_order(normed2_low, core)
    back = Plane(
        [
            [("far down", 0)],
            [("down", 0)],
            [("far gate", 0), ("far down", 1)],
            [("gate", 0), ("down", 1)],
            [("far up", 0), ("far gate", 1)],
            [("up", 0), ("gate", 1)],
            [("far output", 0), ("far up", 1)],
            [("output", 0), ("up", 1)],
            [("far qkv", 0), ("far output", 1)],
            [("qkv", 0), ("output", 1)],
            [("far qkv", 1)],
            [("qkv", 1)],
        ],
        reverse=True,
    )
    sums = back.phases
    sums["far down"], sums["down"] = halves([(cot_core, hidden_low)])
    down_rows = sums["far down"].rows, sums["down"].rows
    seen.D = down_rows

    def go(key):
        first = getattr(Order, key)(seen)
        back.slot(*[y for y in first if not (isinstance(y, tuple) and not y)])
        setattr(seen, key, back.done[-1])

    def far_sum(name, key):
        return swap(after(sums["far " + name].rows.astype(BF16), key), "dp")

    go("b0")
    go("b1")
    grad_result, gate, upward, full_gate, full_up = after(
        tie((cot_both, gate, upward, full_gate, full_up), w_dn, down_rows), Order.hidden
    )
    grad_hidden = matmul(grad_result, w_dn)
    sigma = jax.nn.sigmoid(gate)
    gate_low = (grad_hidden * upward * sigma * (1.0 + gate * (1.0 - sigma))).astype(BF16)
    upward_low = (grad_hidden * gate * sigma).astype(BF16)
    sums["far gate"], sums["gate"] = halves([(normed2_core, after(gate_low, Order.G_dots))])
    seen.G = sums["far gate"].rows, sums["gate"].rows
    part = times_back(after(gate_low, Order.part_gate), full_gate) + times_back(
        after(upward_low, Order.part_up), full_up
    )
    chip_sum = core_sum(part, core)
    seen.chip2 = chip_sum
    head_part = exchange(chip_sum, "pieces_b")
    seen.head2 = head_part
    sums["far up"], sums["up"] = halves([(normed2_core, after(upward_low, Order.U_dots))])
    seen.U = sums["far up"].rows, sums["up"].rows
    go("b2")
    go("b3")
    feed_chip = core_sum(times_back(after(hidden_low, Order.feed), w_dn), core)
    seen.feed = feed_chip
    go("b4")
    feed_head = swap(after(feed_chip, Order.feed_head), "head")
    grad_normed2 = chip_sum.astype(F32) + after(head_part, Order.norm2).astype(F32)
    middle_grad, grad_mlp_gain = norm2_back(grad_normed2)
    grad_middle = cot.astype(F32) + middle_grad
    middle_low = both(grad_middle.astype(BF16), core)
    seen.middle = middle_low
    grad_gated = matmul(after(middle_low, Order.gated), w_out)
    mixed_gradient, outgate_grad, head_gain_part = gated_back(grad_gated)
    outgate_low = outgate_grad.astype(BF16)
    middle_core = core_order(middle_low, core)
    contribution = dot(mixed_gradient, lifted, (0, 0), PASSES)
    seen.contribution = contribution
    go("b5")
    outgoing = incoming(edge, contribution, reverse=True)
    seen.outgoing = outgoing
    far_sums = {}
    if bits == 2:
        far_sums["down"], far_sums["gate"] = far_sum("down", Order.dp_D), far_sum("gate", Order.dp_G)
        seen.D_sum, seen.G_sum = far_sums["down"], far_sums["gate"]
    outgate_late = after(outgate_low, Order.O_dots)
    sums["far output"], sums["output"] = halves(
        [(middle_core, gated_low), (normed_core, outgate_late)]
    )
    seen.O = sums["far output"].rows, sums["output"].rows
    if bits == 2:
        go("b6")
    outgoing = after(outgoing, Order.kernel)
    qkv_low, decay_grad = mixer_backward(
        projected, decay, mixed_gradient, states, fades, incoming_state, outgoing
    )
    logit_low = (decay_grad * jax.nn.sigmoid(-logit) / normalizer).astype(BF16)
    grad_rate = inner(rank_part, logit_low)
    grad_rate_bias = jnp.sum(logit_low.astype(F32), axis=0)
    rank_low = times_back(logit_low, rate).astype(BF16)
    rank_low = jnp.pad(rank_low, ((0, 0), (0, 128 - rank)))
    mixer_low = jnp.concatenate([qkv_low, outgate_low, rank_low], 1)
    seen.qkv = qkv_low
    normed_chip = core_sum(times_back(after(mixer_low, Order.normed), w_mixer), core)
    seen.chip3 = normed_chip
    normed_head = exchange(normed_chip, "pieces_c")
    seen.head3 = normed_head
    qkv_rank = after(jnp.concatenate([qkv_low, rank_low], 1), Order.Q_dots)
    feed_head = after(feed_head, Order.result)
    result = (middle + (feed_chip.astype(F32) + feed_head.astype(F32))).astype(BF16)
    result = reorder(back_place, result)[0]
    seen.result_ = result
    sums["far qkv"], sums["qkv"] = halves([(normed_core, qkv_rank)])
    seen.Q = sums["far qkv"].rows, sums["qkv"].rows
    if bits == 2:
        go("b7")
    go("b8")
    go("b9")
    go("b10")
    if bits == 2:
        far_sums["qkv"] = far_sum("qkv", Order.dp_Q)
        seen.Q_sum = far_sums["qkv"]
    go("b11")
    back.until(*sums)
    if bits == 2:
        far_sums["up"], far_sums["output"] = far_sum("up", Order.dp_U), far_sum("output", Order.dp_O)
        seen.U_sum, seen.O_sum = far_sums["up"], far_sums["output"]
    normed_head = after(normed_head, Order.tail)
    grad_normed = normed_chip.astype(F32) + normed_head.astype(F32)
    inputs_grad, grad_mix_gain = norm_back(grad_normed)
    grad_tokens = reorder(back_place, grad_middle + inputs_grad)[0]

    finished = []
    for name in ("down", "gate", "up", "output", "qkv"):
        got = far_sums[name] if name in far_sums else far_sum(name, Order.rest)
        got = after(got, getattr(Order, "end_" + name))
        finished.append(sums[name].rows.astype(F32) + got.astype(F32))
    grad_down, grad_gate, grad_up, grad_output, grad_qkv = finished

    def own_rows(chip_rows):
        mine = jnp.where(core == 0, chip_rows[:wide], chip_rows[wide:])
        theirs = jnp.where(core == 0, chip_rows[wide:], chip_rows[:wide])
        got = swap(theirs.astype(BF16), "seq", CORE).astype(F32)
        return jnp.where(core == 0, mine, got), jnp.where(core == 0, got, mine)

    def columns(pair, start, width):
        return jnp.concatenate([part[:, start : start + width] for part in pair], 1)

    qkv_pair = own_rows(grad_qkv[:, : 2 * KD + VD])
    sum_query = columns(qkv_pair, 0, KD)
    sum_key = columns(qkv_pair, KD, KD)
    sum_value = columns(qkv_pair, 2 * KD, VD)
    low_rows = grad_qkv[:, 2 * KD + VD : 2 * KD + VD + rank]
    low_mine = jnp.where(core == 0, low_rows[:wide], low_rows[wide:])
    low_theirs = jnp.where(core == 0, low_rows[wide:], low_rows[:wide])
    low_mine = low_mine + swap(low_theirs, "seq", CORE)
    sum_lowrank = low_mine + swap(low_mine, "head")
    output_pair = own_rows(grad_output)
    sum_output = columns(output_pair, 0, VD).T
    sum_outgate = columns(output_pair, VD, VD)
    sum_gate = jnp.concatenate(own_rows(grad_gate), 1)
    sum_up = jnp.concatenate(own_rows(grad_up), 1)
    sum_down = jnp.concatenate(own_rows(grad_down), 1).T

    zero = jnp.zeros_like(grad_rate)
    wide_rate = jnp.where(
        core == 0,
        jnp.concatenate([grad_rate, zero], 1),
        jnp.concatenate([zero, grad_rate], 1),
    )
    wide_bias = jnp.where(
        core == 0,
        jnp.concatenate([grad_rate_bias, zero[0]]),
        jnp.concatenate([zero[0], grad_rate_bias]),
    )
    head_gain_part = head_gain_part + swap(head_gain_part[None], "head")[0]
    gain_rows = jnp.stack([grad_mix_gain, grad_mlp_gain])
    gain_rows = reorder(back_place, jnp.pad(gain_rows, ((0, 6), (0, 0))))[0][:2]
    model = gain_rows.shape[1]
    others = jnp.concatenate([wide_bias, head_gain_part])
    others = jnp.pad(others, (0, 2 * model - others.shape[0])).reshape(2, model)
    others = jnp.concatenate([others, wide_rate.reshape(-1, model)], 0)
    small = jnp.concatenate([gain_rows, others], 0)
    for axis, axis_bits in (("seq", [CORE] + chip_bits()), ("dp", [1])):
        for bit in axis_bits:
            small = small + swap(small, axis, bit)
    sum_mix_gain, sum_mlp_gain = small[0], small[1]
    sum_rate_bias = small[2, : wide_bias.size]
    sum_head_gain = small[2, wide_bias.size : wide_bias.size + VD]
    sum_rate = small[4:].reshape(wide_rate.shape)
    return (
        result,
        grad_tokens,
        sum_mix_gain,
        sum_query,
        sum_key,
        sum_value,
        sum_outgate,
        sum_lowrank,
        sum_rate,
        sum_rate_bias,
        sum_head_gain,
        sum_output,
        sum_mlp_gain,
        sum_gate,
        sum_up,
        sum_down,
    )


def solution(mesh):
    rows = P(("dp", "seq"), None)
    in_columns = P(("dp", "seq"), "head")
    in_rows = P("head", ("dp", "seq"))
    in_specs = (
        rows,
        P(),
        in_columns,
        in_columns,
        in_columns,
        in_columns,
        rows,
        P(None, "head"),
        P("head"),
        P(),
        in_rows,
        P(),
        in_columns,
        in_columns,
        in_rows,
        rows,
    )
    out_specs = (
        rows,
        rows,
        P(),
        in_columns,
        in_columns,
        in_columns,
        in_columns,
        rows,
        P(None, "head"),
        P("head"),
        P(),
        in_rows,
        P(),
        in_columns,
        in_columns,
        in_rows,
    )
    return jax.shard_map(body, mesh=mesh, in_specs=in_specs, out_specs=out_specs, check_vma=False)
```
